128 devices in a mesh: section: 4 (over y), group: 32 (over x, z, core).
Axes of the slice: x: 4, y: 4, z: 4, core: 2. Of those that a mesh axis runs over, the one named last changes fastest.
Arguments:
- hidden: bfloat16 [256, 4096], P(('section', 'group')), may hold values from -16 to 16
- targets: int32 [256], P(('section', 'group')), may hold values from 0 to 131071
- token_weight: bfloat16 [256], P(('section', 'group')), may hold values from 2 to 32
- head_weight: bfloat16 [131072, 4096], P(('section', 'group')), may hold values from -0.5 to 0.5
- token_ids: int32 [256], P(('section', 'group')), may hold values from 0 to 131071
- embed_cotangent: bfloat16 [256, 4096], P(('section', 'group')), may hold values from -6 to 6
- new_rows: int32 [8, 2], replicated, may hold values from 0 to 131072, as said below
Outputs:
- mean_loss: float32 [], replicated
- grad_hidden: bfloat16 [256, 4096], P('section', 'group')
- grad_head: bfloat16 [131072, 4096], P(('section', 'group'))
- grad_embed: bfloat16 [131072, 4096], P(('section', 'group'))
The draws below stay inside these ranges and needn't reach their ends.
Inputs may be any that keep to these rules, and one draw needn't show every extreme that they name: `new_rows`: 8 disjoint ascending ranges [start, end) with start < end; the first starts at 0 and the last ends at 131072.
All inputs are finite; a program needn't handle non-finite values.
Results may differ from the reference program's by a relative error of at most 0.0095.
Values may be sent and summed in bfloat16 or wider, within the bound.
No kernel may reach another device: no remote copies, remote signals or barrier semaphores. Data moves between devices by JAX's collectives and lax.ppermute only.
A program may use at most 128 MiB of HBM per device.

```python
import math
import jax
import jax.numpy as jnp
import numpy as np
from jax import lax

D = 4096
VOC_DEV = 1024
TOKENS = 256
RANGES = 8
VOCAB = 131072
N_SECTION = 4
N_GROUP = 32


def common_pair(key):
    table = jax.random.normal(jax.random.fold_in(key, 11), (VOCAB, D), jnp.float32) * (3.0 / math.sqrt(D))
    table = jnp.clip(table, -0.5, 0.5)
    states = jax.random.normal(jax.random.fold_in(key, 12), (TOKENS, D), jnp.float32)
    return (table, states)


def draw_head_weight(key, part):
    table, states = common_pair(key)
    return table.astype(jnp.bfloat16)


def draw_hidden(key, part):
    table, states = common_pair(key)
    states = jnp.clip(states, -16.0, 16.0)
    return states.astype(jnp.bfloat16)


def draw_new_rows(key, part):
    key = jax.random.fold_in(key, 5)
    segment = VOCAB // RANGES
    first_key, second_key = jax.random.split(key)
    index = jnp.arange(RANGES, dtype=jnp.int32)
    offset = jax.random.randint(first_key, (RANGES,), 0, segment // 2)
    length = jax.random.randint(second_key, (RANGES,), segment // 4, segment // 2 + 1)
    range_start = jnp.where(index == 0, 0, index * segment + offset)
    range_end = jnp.minimum(range_start + length, (index + 1) * segment)
    range_end = jnp.where(index == RANGES - 1, VOCAB, range_end)
    return jnp.stack([range_start, range_end], axis=1).astype(jnp.int32)


def touch_ends(drawn, stream_key, least, high):
    index_at = [jax.random.randint(jax.random.fold_in(stream_key, axis), (), 0, length) for axis, length in enumerate(drawn.shape)]
    widest = drawn.shape.index(max(drawn.shape))
    neighbour = index_at[:widest] + [(index_at[widest] + 1) % drawn.shape[widest]] + index_at[widest + 1:]
    return drawn.at[tuple(index_at)].set(least).at[tuple(neighbour)].set(high)


def block_scale(stream_key, extent, cuts, least, high):
    def one(position, parts):
        steps = jax.random.uniform(jax.random.fold_in(jax.random.fold_in(stream_key, 6), position), (parts,), jnp.float32, least / len(cuts), high / len(cuts))
        return jnp.repeat(jnp.exp(steps), extent[position] // parts).reshape((-1,) + (1,) * (len(extent) - position - 1))

    gain = one(*cuts[0])
    for cut in cuts[1:]:
        gain = gain * one(*cut)
    return gain


def wide_ids(own_key, dims, count, skew):
    loads = [min(1 << octave, count + 1 - (1 << octave)) * (1 << 20) // math.isqrt((1 << octave) ** skew) + 1 for octave in range((count + 1).bit_length()) if 1 << octave <= count]
    deviation = 1 + sum(loads) // (1 << 30)
    listing = np.cumsum(np.array([max(1, weight // deviation) for weight in loads]))
    lot = jax.random.randint(jax.random.fold_in(own_key, 1), dims, 0, int(listing[len(loads) - 1]))
    start = jnp.left_shift(1, jnp.searchsorted(jnp.asarray(listing, jnp.int32), lot, side="right").astype(jnp.int32))
    grade = start - 1 + jax.random.randint(jax.random.fold_in(own_key, 4), dims, 0, 1 << 30) % jnp.minimum(start, count + 1 - start)
    return jax.random.permutation(jax.random.fold_in(own_key, 2), count)[grade].astype(jnp.int32)


def normal_values(own_key, shape, deviation, bound, pieces=(), held_as=jnp.bfloat16):
    array = deviation * jax.random.normal(own_key, shape, jnp.float32)
    if pieces:
        array = array * block_scale(own_key, shape, pieces, -0.22, 0.18)
    return jnp.clip(array, -bound, bound).astype(held_as)


def setup_inputs(seed: int = 0) -> dict:
    arg_keys = jax.random.split(jax.random.key(seed), 8)
    return {
        "hidden": draw_hidden(jax.random.fold_in(arg_keys[7], 71), 0),
        "targets": touch_ends(wide_ids(arg_keys[1], (TOKENS,), VOCAB, 2), jax.random.fold_in(arg_keys[1], 3), 0, VOCAB - 1).astype(jnp.int32),
        "token_weight": jnp.clip(jnp.exp(math.log(32.0) - 2.7725887 * jax.random.uniform(arg_keys[2], (TOKENS,), jnp.float32) ** block_scale(arg_keys[2], (TOKENS,), ((0, 128),), -0.2, 0.2)), 2.0, 32.0).astype(jnp.bfloat16),
        "head_weight": draw_head_weight(jax.random.fold_in(arg_keys[7], 71), 0),
        "token_ids": touch_ends(wide_ids(arg_keys[4], (TOKENS,), VOCAB, 2), jax.random.fold_in(arg_keys[4], 3), 0, VOCAB - 1).astype(jnp.int32),
        "embed_cotangent": normal_values(arg_keys[5], (TOKENS, D), 1.0, 6.0, ((0, 128),)),
        "new_rows": draw_new_rows(jax.random.fold_in(arg_keys[7], 71), 0),
    }


def reference(hidden, targets, token_weight, head_weight, token_ids, embed_cotangent, new_rows):
    logits = lax.dot_general(hidden, head_weight, (((1,), (1,)), ((), ())), preferred_element_type=jnp.float32)
    row_peak = jnp.max(logits, axis=1)
    exp_total = jnp.sum(jnp.exp(logits - row_peak[:, None]), axis=1)
    picked = jnp.take_along_axis(logits, targets[:, None].astype(jnp.int32), axis=1)[:, 0]
    log_norm = row_peak + jnp.log(exp_total)
    weights = token_weight.astype(jnp.float32)
    mean_loss = jnp.sum(weights * (log_norm - picked)) / jnp.sum(weights)
    target_hits = (targets[:, None] == jnp.arange(VOCAB, dtype=jnp.int32)[None, :]).astype(jnp.float32)
    slopes = (weights[:, None] * (jnp.exp(logits - log_norm[:, None]) - target_hits)).astype(jnp.bfloat16)
    grad_hidden = jnp.dot(slopes, head_weight, preferred_element_type=jnp.float32).astype(jnp.bfloat16)

    def per_block(block):
        row_start = block * VOC_DEV
        row_ids = row_start + jnp.arange(VOC_DEV, dtype=jnp.int32)
        inside = (row_ids[:, None] >= new_rows[None, :, 0]) & (row_ids[:, None] < new_rows[None, :, 1])
        keep_gate = jnp.any(inside, axis=1).astype(jnp.float32)[:, None]
        block_slopes = lax.dynamic_slice_in_dim(slopes, row_start, VOC_DEV, 1)
        head_part = lax.dot_general(block_slopes, hidden, (((0,), (0,)), ((), ())), preferred_element_type=jnp.float32)
        onehot = (token_ids[:, None] == row_ids[None, :]).astype(jnp.bfloat16)
        embed_part = lax.dot_general(onehot, embed_cotangent, (((0,), (0,)), ((), ())), preferred_element_type=jnp.float32)
        return (head_part * keep_gate).astype(jnp.bfloat16), (embed_part * keep_gate).astype(jnp.bfloat16)

    blocks = jnp.arange(N_SECTION * N_GROUP, dtype=jnp.int32)
    head_blocks, embed_blocks = lax.map(per_block, blocks)
    grad_head = head_blocks.reshape(VOCAB, D)
    grad_embed = embed_blocks.reshape(VOCAB, D)
    return mean_loss, grad_hidden, grad_head, grad_embed
```

```python
import jax
import jax.numpy as jnp
from jax import lax
from jax.experimental import pallas as pl
from jax.experimental.pallas import tpu as pltpu
from jax.sharding import Mesh, PartitionSpec as P

CHIPS = ("y", "x", "z")
ALL = ("y", "x", "z", "c")
LANES = 128


def swap_cores(value):
    return lax.ppermute(value, "c", [(0, 1), (1, 0)])


def encode_ids(ids):
    digits = [(ids >> 12) & 63, (ids >> 6) & 63, ids & 63]
    return [digit.astype(jnp.bfloat16) for digit in digits]


def decode_ids(digits):
    high, mid, low = (digits[:, place].astype(jnp.int32) for place in range(3))
    return (high << 12) + (mid << 6) + low


def feature_partials(core, slopes, head_weight):
    tokens, rows = slopes.shape
    width = head_weight.shape[1]
    blocks = width // (2 * LANES)

    def kernel(core_ref, slopes_ref, first_ref, second_ref, out_ref):
        pair = jnp.concatenate([first_ref[...], second_ref[...]], axis=1)
        total = jnp.dot(slopes_ref[...], pair, preferred_element_type=jnp.float32)
        total = total.astype(jnp.bfloat16)
        out_ref[0] = total[:, :LANES]
        out_ref[1] = total[:, LANES:]

    return pl.pallas_call(
        kernel,
        out_shape=jax.ShapeDtypeStruct((blocks, tokens, LANES), jnp.bfloat16),
        grid_spec=pltpu.PrefetchScalarGridSpec(
            num_scalar_prefetch=1,
            grid=(blocks // 2,),
            in_specs=[
                pl.BlockSpec((tokens, rows), lambda i, core: (0, 0)),
                pl.BlockSpec((rows, LANES), lambda i, core: (0, 4 * i + core[0])),
                pl.BlockSpec((rows, LANES), lambda i, core: (0, 4 * i + 2 + core[0])),
            ],
            out_specs=pl.BlockSpec((2, tokens, LANES), lambda i, core: (i, 0, 0)),
        ),
        compiler_params=pltpu.CompilerParams(vmem_limit_bytes=16 * 1024 * 1024),
        cost_estimate=pl.CostEstimate(
            flops=tokens * rows * width,
            bytes_accessed=rows * width + tokens * rows * 2 + tokens * width,
            transcendentals=0,
        ),
    )(core, slopes, head_weight, head_weight)


def local(hidden, targets, token_weight, head_weight, token_ids, embed_cotangent, new_rows):
    core = lax.axis_index("c")
    chips = lax.axis_size("y") * lax.axis_size("x") * lax.axis_size("z")
    devices = 2 * chips
    held, width = hidden.shape
    half = width // 2
    tokens = held * devices
    voc_rows = head_weight.shape[0]

    all_cotangent = lax.all_gather(embed_cotangent, ALL, axis=0, tiled=True)

    meta = jnp.stack(
        encode_ids(targets) + encode_ids(token_ids) + [token_weight], axis=1
    )
    meta = jnp.pad(meta, ((0, 0), (0, LANES - meta.shape[1])))
    low, high = hidden[:, :half], hidden[:, half:]
    mine = jnp.concatenate([jnp.where(core == 0, low, high), meta], axis=1)
    theirs = jnp.concatenate([jnp.where(core == 0, high, low), meta], axis=1)
    theirs = swap_cores(theirs)
    block = jnp.where(
        core == 0,
        jnp.concatenate([mine, theirs], axis=0),
        jnp.concatenate([theirs, mine], axis=0),
    )
    block = jnp.broadcast_to(block[None], (chips,) + block.shape)
    gathered = lax.all_to_all(block, CHIPS, 0, 0, tiled=True)
    near = gathered[:, :, :half]
    far = swap_cores(near)
    near, far = near.reshape(tokens, half), far.reshape(tokens, half)
    all_hidden = jnp.where(
        core == 0,
        jnp.concatenate([near, far], axis=1),
        jnp.concatenate([far, near], axis=1),
    )
    all_meta = gathered[:, :, half:].reshape(tokens, LANES)
    all_targets = decode_ids(all_meta[:, 0:3])
    all_ids = decode_ids(all_meta[:, 3:6])
    weights = all_meta[:, 6].astype(jnp.float32)

    device = ((lax.axis_index("y") * lax.axis_size("x") + lax.axis_index("x"))
              * lax.axis_size("z") + lax.axis_index("z")) * 2 + core
    row_ids = device * voc_rows + jnp.arange(voc_rows, dtype=jnp.int32)
    inside = (row_ids[:, None] >= new_rows[None, :, 0]) & (row_ids[:, None] < new_rows[None, :, 1])
    trainable = jnp.any(inside, axis=1)

    logits = lax.dot_general(
        all_hidden, head_weight, (((1,), (1,)), ((), ())), preferred_element_type=jnp.float32
    )
    target_hits = all_targets[:, None] == row_ids[None, :]
    peak_local = jnp.max(logits, axis=1)
    total_local = jnp.sum(jnp.exp(logits - peak_local[:, None]), axis=1)
    picked_local = jnp.sum(jnp.where(target_hits, logits, 0.0), axis=1)

    stats = jnp.concatenate([peak_local, total_local, picked_local])
    stats = jnp.broadcast_to(stats[None, None], (devices, 1, 3 * tokens))
    stats = lax.all_to_all(stats, ALL, 0, 0, tiled=True)[:, 0]
    peaks, totals, picks = stats[:, :tokens], stats[:, tokens:2 * tokens], stats[:, 2 * tokens:]
    row_peak = jnp.max(peaks, axis=0)
    exp_total = jnp.sum(totals * jnp.exp(peaks - row_peak[None]), axis=0)
    picked = jnp.sum(picks, axis=0)
    log_norm = row_peak + jnp.log(exp_total)
    mean_loss = jnp.sum(weights * (log_norm - picked)) / jnp.sum(weights)

    slopes = (
        weights[:, None] * (jnp.exp(logits - log_norm[:, None]) - target_hits.astype(jnp.float32))
    ).astype(jnp.bfloat16)

    away = feature_partials((1 - core)[None].astype(jnp.int32), slopes, head_weight)
    away = swap_cores(away)
    home = feature_partials(core[None].astype(jnp.int32), slopes, head_weight)
    pair = (home.astype(jnp.float32) + away.astype(jnp.float32)).astype(jnp.bfloat16)
    sections = lax.axis_size("y")
    owned = tokens // sections
    pair = pair.reshape(chips // sections, sections, owned, LANES).transpose(1, 0, 2, 3)
    pair = pair.reshape(chips, owned, LANES)
    parts = lax.all_to_all(pair, CHIPS, 0, 0, tiled=True)
    grad_hidden = jnp.sum(parts.astype(jnp.float32), axis=0).astype(jnp.bfloat16)

    gate = trainable[None, :]
    head_slopes = jnp.where(gate, slopes, jnp.zeros_like(slopes))
    grad_head = lax.dot_general(
        head_slopes, all_hidden, (((0,), (0,)), ((), ())), preferred_element_type=jnp.float32
    ).astype(jnp.bfloat16)
    onehot = ((all_ids[:, None] == row_ids[None, :]) & gate).astype(jnp.bfloat16)
    grad_embed = lax.dot_general(
        onehot, all_cotangent, (((0,), (0,)), ((), ())), preferred_element_type=jnp.float32
    ).astype(jnp.bfloat16)
    return (mean_loss, grad_hidden, grad_head, grad_embed)


def solution(mesh):
    grid = Mesh(mesh.devices.reshape(4, 4, 4, 2), ALL)
    rows = P(ALL)
    in_specs = (P(ALL, None), rows, rows, P(ALL, None), rows, P(ALL, None), P())
    out_specs = (P(), P("y", ("x", "z", "c")), P(ALL, None), P(ALL, None))
    return jax.shard_map(local, mesh=grid, in_specs=in_specs, out_specs=out_specs, check_vma=False)
```

```python
import jax
import jax.numpy as jnp
from jax import lax
from jax.experimental import pallas as pl
from jax.experimental.pallas import tpu as pltpu
from jax.sharding import Mesh, PartitionSpec as P

CHIPS = ("y", "x", "z")
ALL = ("y", "x", "z", "c")
LANES = 128
VMEM_LIMIT = 24 * 1024 * 1024
F32, BF16, I32 = jnp.float32, jnp.bfloat16, jnp.int32
NT = (((1,), (1,)), ((), ()))
WHOLE = pl.BlockSpec(memory_space=pltpu.VMEM)
IN_HBM = pl.BlockSpec(memory_space=pltpu.HBM)


def call(kernel, name, out_shape, grid, in_specs, out_specs, scratch, flops, moved, scalars, *arrays):
    return pl.pallas_call(
        kernel,
        name=name,
        out_shape=out_shape,
        grid_spec=pltpu.PrefetchScalarGridSpec(
            num_scalar_prefetch=len(scalars),
            grid=grid,
            in_specs=in_specs,
            out_specs=out_specs,
            scratch_shapes=scratch,
        ),
        compiler_params=pltpu.CompilerParams(vmem_limit_bytes=VMEM_LIMIT),
        cost_estimate=pl.CostEstimate(flops=flops, bytes_accessed=moved, transcendentals=0),
    )(*scalars, *arrays)


def in_hbm(value):
    return pltpu.with_memory_space_constraint(value, pltpu.HBM)


def swap_cores(value):
    return lax.ppermute(value, "c", [(0, 1), (1, 0)])


def own_block(core, targets, weights, ids, hidden, cotangent):
    held, width = hidden.shape
    half = width // 2

    def kernel(core_ref, targets_hbm, weights_ref, ids_hbm, hidden_hbm, cotangent_hbm, mine_ref, theirs_ref,
               targets_ref, ids_ref, hidden_ref, cotangent_ref, sems):
        pairs = [(targets_hbm, targets_ref), (ids_hbm, ids_ref),
                 (hidden_hbm, hidden_ref), (cotangent_hbm, cotangent_ref)]
        copies = [pltpu.make_async_copy(source, target, sems.at[place])
                  for place, (source, target) in enumerate(pairs)]
        for copy in copies:
            copy.start()
        for copy in copies:
            copy.wait()
        row = lax.broadcasted_iota(I32, (held, LANES), 0)
        lane = lax.broadcasted_iota(I32, (held, LANES), 1)
        meta = jnp.zeros((held, LANES), F32)
        for token in range(held):
            target, name = targets_ref[token], ids_ref[token]
            values = [(target >> 12) & 63, (target >> 6) & 63, target & 63,
                      (name >> 12) & 63, (name >> 6) & 63, name & 63]
            values = [value.astype(F32) for value in values] + [weights_ref[token]]
            for place, value in enumerate(values):
                meta = jnp.where((row == token) & (lane == place), value, meta)
        meta = meta.astype(BF16)
        low = jnp.concatenate([hidden_ref[:, :half], meta, cotangent_ref[:, :half]], axis=1)
        high = jnp.concatenate([hidden_ref[:, half:], meta, cotangent_ref[:, half:]], axis=1)

        @pl.when(core_ref[0] == 0)
        def _():
            mine_ref[...] = low
            theirs_ref[...] = high

        @pl.when(core_ref[0] == 1)
        def _():
            mine_ref[...] = high
            theirs_ref[...] = low

    shape = jax.ShapeDtypeStruct((held, width + LANES), BF16)
    return call(
        kernel, "own_block", [shape, shape], (),
        [IN_HBM, pl.BlockSpec(memory_space=pltpu.SMEM), IN_HBM, IN_HBM, IN_HBM], [WHOLE] * 2,
        [
            pltpu.SMEM((held,), I32), pltpu.SMEM((held,), I32),
            pltpu.VMEM((held, width), BF16), pltpu.VMEM((held, width), BF16),
            pltpu.SemaphoreType.DMA((4,)),
        ], 0, 8 * held * width, [core],
        in_hbm(targets), weights, in_hbm(ids), in_hbm(hidden), in_hbm(cotangent),
    )


def chip_blocks(core, chips, mine, theirs):
    held, width = mine.shape

    def kernel(core_ref, mine_ref, theirs_ref, out_ref):
        own, other = mine_ref[...].astype(F32), theirs_ref[...].astype(F32)
        first = core_ref[0] == 0
        both = jnp.concatenate([jnp.where(first, own, other), jnp.where(first, other, own)], axis=0).astype(BF16)
        out_ref[...] = jnp.broadcast_to(both[None], out_ref.shape)

    return call(
        kernel, "chip_blocks", jax.ShapeDtypeStruct((chips, 2 * held, width), BF16), (),
        [WHOLE] * 2, WHOLE, [], 0, 4 * chips * held * width, [core], mine, theirs,
    )


def token_rows(gathered):
    chips, held, width = gathered.shape
    tokens, half = chips * held, (width - LANES) // 2

    def kernel(gathered_ref, hidden_ref, cotangent_ref, info_ref):
        hidden_ref[...] = gathered_ref[:, :, :half].reshape(tokens, half)
        cotangent_ref[...] = gathered_ref[:, :, half + LANES:].reshape(tokens, half)
        rows = jnp.transpose(gathered_ref[:, :, half:half + LANES].reshape(tokens, LANES).astype(F32))
        targets = rows[0:1] * 4096.0 + rows[1:2] * 64.0 + rows[2:3]
        ids = rows[3:4] * 4096.0 + rows[4:5] * 64.0 + rows[5:6]
        info_ref[...] = jnp.concatenate([targets, ids, rows[6:7], jnp.zeros((5, tokens), F32)], axis=0)

    shape = jax.ShapeDtypeStruct((tokens, half), BF16)
    return call(
        kernel, "token_rows", [shape, shape, jax.ShapeDtypeStruct((8, tokens), F32)],
        (), [WHOLE], [WHOLE] * 3, [], 0, 4 * tokens * width, [], gathered,
    )


def near_logits(core, gathered, head_weight):
    tokens = gathered.shape[0]
    rows, width = head_weight.shape
    half, step = width // 2, 256

    def kernel(core_ref, gathered_ref, head_hbm, out_ref, head_ref, sems):
        copies = [
            pltpu.make_async_copy(
                head_hbm.at[pl.ds(place, step)], head_ref.at[pl.ds(place, step)], sems.at[place // step])
            for place in range(0, rows, step)]
        for copy in copies:
            copy.start()
        columns = pl.ds(pl.multiple_of(core_ref[0] * half, half), half)
        for copy, place in zip(copies, range(0, rows, step)):
            copy.wait()
            out_ref[place:place + step, :] = lax.dot_general(
                head_ref[place:place + step, columns], gathered_ref[:, :half], NT, preferred_element_type=F32)

    return call(
        kernel, "near_logits",
        [jax.ShapeDtypeStruct((rows, tokens), F32), pltpu.VMEM((rows, width), BF16)],
        (), [WHOLE, IN_HBM], [WHOLE] * 2,
        [pltpu.SemaphoreType.DMA((rows // step,))],
        2 * tokens * rows * half, 4 * rows * half, [core], gathered, in_hbm(head_weight),
    )


def feature_products(side, left_ref, head_ref, first, blocks):
    count = left_ref.shape[0]
    for block in range(first, first + blocks, 2):
        columns = jnp.concatenate([
            head_ref[:, pl.ds(pl.multiple_of((2 * place + side) * LANES, LANES), LANES)]
            for place in (block, block + 1)], axis=1)
        for line in range(0, count, count // 2):
            lines = slice(line, line + count // 2)
            total = jnp.dot(left_ref[lines, :], columns, preferred_element_type=F32).astype(BF16)
            yield block, lines, total[:, :LANES], total[:, LANES:]


def far_logits(core, start, devices, partial, info, gathered, head_weight):
    tokens = gathered.shape[0]
    rows, width = head_weight.shape
    half, step = width // 2, 256
    blocks = half // LANES

    def kernel(core_ref, start_ref, partial_ref, info_ref, gathered_ref, head_ref,
               logits_hbm, stats_hbm, left_hbm, away_hbm,
               logits_ref, stats_ref, left_ref, away_ref, sems, away_sems):
        other = 1 - core_ref[0]
        columns = pl.ds(pl.multiple_of(other * half, half), half)
        for place in range(0, rows, step):
            logits_ref[place:place + step, :] = partial_ref[place:place + step, :] + lax.dot_general(
                head_ref[place:place + step, columns], gathered_ref[:, :half], NT, preferred_element_type=F32)
        copies = [pltpu.make_async_copy(logits_ref, logits_hbm, sems.at[0])]
        copies[-1].start()
        logits = logits_ref[...]
        peak = jnp.max(logits, axis=0, keepdims=True)
        powers = jnp.exp(logits - peak)
        total = jnp.sum(powers, axis=0, keepdims=True)
        row = lax.broadcasted_iota(I32, (rows, tokens), 0) + start_ref[0]
        hits = row == info_ref[0:1, :].astype(I32)
        picked = jnp.sum(jnp.where(hits, logits, 0.0), axis=0, keepdims=True)
        parts = [value[:, place:place + LANES] for value in (peak, total, picked) for place in range(0, tokens, LANES)]
        block = jnp.concatenate(parts + [jnp.zeros((8 - len(parts), LANES), F32)], axis=0)
        stats_ref[...] = jnp.broadcast_to(block[None], stats_ref.shape)
        copies.append(pltpu.make_async_copy(stats_ref, stats_hbm, sems.at[1]))
        copies[-1].start()
        left_ref[:tokens, :] = jnp.transpose(jnp.where(hits, 0.0, powers)).astype(BF16)
        left_ref[tokens:, :] = jnp.transpose(hits.astype(F32)).astype(BF16)
        copies.append(pltpu.make_async_copy(left_ref, left_hbm, sems.at[2]))
        copies[-1].start()
        for first in range(0, blocks, 4):
            for block, lines, even, odd in feature_products(other, left_ref, head_ref, first, 4):
                away_ref[block, lines, :] = even
                away_ref[block + 1, lines, :] = odd
            part = pl.ds(first, 4)
            copies.append(pltpu.make_async_copy(away_ref.at[part], away_hbm.at[part], away_sems.at[first // 4]))
            copies[-1].start()
        for copy in copies:
            copy.wait()

    shapes = [
        ((rows, tokens), F32), ((devices, 8, LANES), F32),
        ((2 * tokens, rows), BF16), ((blocks, 2 * tokens, LANES), BF16),
    ]
    return call(
        kernel, "far_logits", [pltpu.HBM(*shape) for shape in shapes],
        (), [WHOLE] * 4, [IN_HBM] * 4,
        [pltpu.VMEM(*shape) for shape in shapes]
        + [pltpu.SemaphoreType.DMA((3,)), pltpu.SemaphoreType.DMA((blocks // 4,))],
        6 * tokens * rows * half, 2 * rows * half, [core, start], partial, info, gathered, head_weight,
    )


def feature_partials(core, left, head_weight):
    count, rows = left.shape
    width = head_weight.shape[1]
    blocks = width // (2 * LANES)
    step = 1024
    held = step // (2 * LANES)

    def kernel(core_ref, left_ref, head_ref, out_ref):
        for block, lines, even, odd in feature_products(core_ref[0], left_ref, head_ref, 0, held):
            out_ref[block, lines, :] = even
            out_ref[block + 1, lines, :] = odd

    return call(
        kernel, "feature_partials", pltpu.HBM((blocks, count, LANES), BF16), (width // step,),
        [
            pl.BlockSpec((count, rows), lambda i, core: (0, 0)),
            pl.BlockSpec((rows, step), lambda i, core: (0, i)),
        ],
        pl.BlockSpec((held, count, LANES), lambda i, core: (i, 0, 0)),
        [], count * rows * width, 2 * rows * width, [core], in_hbm(left), in_hbm(head_weight),
    )


def scaled_pair(device, stats, info, home, away):
    tokens = info.shape[1]
    blocks = home.shape[0]
    sections = lax.axis_size("y")
    owned = tokens // sections
    lines = tokens // LANES

    def kernel(device_ref, stats_hbm, info_ref, home_hbm, away_hbm, out_hbm, norm_ref, loss_ref,
               stats_ref, home_ref, away_ref, out_ref, stats_sem, in_sems, out_sems):
        stats_copy = pltpu.make_async_copy(stats_hbm, stats_ref, stats_sem)
        stats_copy.start()
        loads = []
        for section in range(sections):
            power = pl.ds(section * owned, owned)
            hit = pl.ds(tokens + section * owned, owned)
            loads.append([
                pltpu.make_async_copy(source.at[:, part, :], target.at[:, part, :], in_sems.at[section, place])
                for place, (source, target, part) in enumerate([
                    (home_hbm, home_ref, power), (away_hbm, away_ref, power),
                    (home_hbm, home_ref, hit), (away_hbm, away_ref, hit)])])
            for load in loads[-1]:
                load.start()

        def flat(block, first):
            return jnp.concatenate([block[first + line:first + line + 1] for line in range(lines)], axis=1)

        stats_copy.wait()
        everyone = stats_ref[...]
        peaks = jnp.max(everyone, axis=0)
        factors = jnp.exp(everyone[:, :lines] - peaks[None, :lines])
        total = jnp.sum(everyone[:, lines:2 * lines] * factors, axis=0)
        picked = flat(jnp.sum(everyone, axis=0), 2 * lines)
        norm = flat(peaks, 0) + jnp.log(flat(total, 0))
        weights = info_ref[2:3, :]
        norm_ref[...] = norm
        loss_ref[...] = (jnp.sum(weights * (norm - picked), axis=1, keepdims=True)
                         / jnp.sum(weights, axis=1, keepdims=True))
        here = device_ref[0]
        own = flat(stats_ref[here], 0)
        other = flat(stats_ref[here + 1 - 2 * (here & 1)], 0)
        scale = jnp.transpose(jnp.concatenate([
            weights * jnp.exp(own - norm),
            weights * jnp.exp(other - norm),
            weights * (jnp.exp(picked - norm) - 1.0),
            jnp.zeros((5, tokens), F32),
        ], axis=0))
        stores = []
        for section in range(sections):
            for load in loads[section]:
                load.wait()
            power = slice(section * owned, (section + 1) * owned)
            hit = slice(tokens + section * owned, tokens + (section + 1) * owned)
            one, two, three = (
                jnp.broadcast_to(scale[power, place:place + 1], (owned, LANES)) for place in range(3))
            for block in range(blocks):
                value = home_ref[block, power, :].astype(F32) * one + away_ref[block, power, :].astype(F32) * two
                hits = (home_ref[block, hit, :] + away_ref[block, hit, :]).astype(F32)
                out_ref[section * blocks + block] = (value + hits * three).astype(BF16)
            part = pl.ds(section * blocks, blocks)
            stores.append(pltpu.make_async_copy(out_ref.at[part], out_hbm.at[part], out_sems.at[section]))
            stores[-1].start()
        for store in stores:
            store.wait()

    return call(
        kernel, "scaled_pair",
        [
            pltpu.HBM((sections * blocks, owned, LANES), BF16),
            jax.ShapeDtypeStruct((1, tokens), F32),
            jax.ShapeDtypeStruct((1, 1), F32),
        ],
        (), [IN_HBM, WHOLE, IN_HBM, IN_HBM], [IN_HBM, WHOLE, WHOLE],
        [
            pltpu.VMEM(stats.shape, F32), pltpu.VMEM(home.shape, BF16), pltpu.VMEM(away.shape, BF16),
            pltpu.VMEM((sections * blocks, owned, LANES), BF16),
            pltpu.SemaphoreType.DMA, pltpu.SemaphoreType.DMA((sections, 4)), pltpu.SemaphoreType.DMA((sections,)),
        ],
        10 * tokens * blocks * LANES, 10 * tokens * blocks * LANES, [device],
        in_hbm(stats), info, in_hbm(home), in_hbm(away),
    )


def summed_parts(parts):
    count, rows, width = parts.shape
    share = count // 4

    def kernel(parts_hbm, out_ref, parts_ref, sems):
        copies = [
            pltpu.make_async_copy(parts_hbm.at[pl.ds(first, share)], parts_ref.at[pl.ds(first, share)], sems.at[place])
            for place, first in enumerate(range(0, count, share))]
        for copy in copies:
            copy.start()
        total = jnp.zeros((rows, width), F32)
        for place, copy in enumerate(copies):
            copy.wait()
            total += jnp.sum(parts_ref[place * share:(place + 1) * share].astype(F32), axis=0)
        out_ref[...] = total.astype(BF16)

    return call(
        kernel, "summed_parts", jax.ShapeDtypeStruct((rows, width), BF16), (), [IN_HBM], WHOLE,
        [pltpu.VMEM(parts.shape, BF16), pltpu.SemaphoreType.DMA((4,))],
        count * rows * width, 2 * count * rows * width, [], in_hbm(parts),
    )


def row_gradient(name, make_left, core, start, new_rows, rows, small, near, far, step=1024):
    tokens = near.shape[0]
    half = near.shape[1]
    steps = half // step

    def kernel(core_ref, start_ref, ranges_ref, *refs):
        small_refs, (near_ref, far_ref, out_ref, left_ref) = refs[:len(small)], refs[len(small):]
        index = pl.program_id(0)

        @pl.when(index == 0)
        def _():
            lane_row = lax.broadcasted_iota(I32, (8, rows), 1) + start_ref[0]
            inside = jnp.zeros((8, rows), F32)
            for place in range(new_rows.shape[0]):
                within = (lane_row >= ranges_ref[place, 0]) & (lane_row < ranges_ref[place, 1])
                inside = jnp.where(within, 1.0, inside)
            gate = jnp.transpose(inside)[:, 0:1]
            row = lax.broadcasted_iota(I32, (rows, tokens), 0) + start_ref[0]
            left_ref[...] = jnp.where(gate > 0.0, make_left(row, *small_refs), 0.0).astype(BF16)

        @pl.when(index < steps)
        def _():
            out_ref[...] = jnp.dot(left_ref[...], near_ref[...], preferred_element_type=F32).astype(BF16)

        @pl.when(index >= steps)
        def _():
            out_ref[...] = jnp.dot(left_ref[...], far_ref[...], preferred_element_type=F32).astype(BF16)

    def out_index(i, core, start, ranges):
        is_far = (i >= steps).astype(I32)
        side = core[0] + is_far - 2 * core[0] * is_far
        return (0, side * steps + i - is_far * steps)

    return call(
        kernel, name,
        jax.ShapeDtypeStruct((rows, 2 * half), BF16),
        (2 * steps,),
        [pl.BlockSpec(array.shape, lambda i, core, start, ranges: (0, 0)) for array in small] + [
            pl.BlockSpec((tokens, step), lambda i, core, start, ranges: (0, jnp.minimum(i, steps - 1))),
            pl.BlockSpec((tokens, step), lambda i, core, start, ranges: (0, jnp.maximum(i - steps, 0))),
        ],
        pl.BlockSpec((rows, step), out_index),
        [pltpu.VMEM((rows, tokens), BF16)],
        4 * rows * tokens * half, 4 * rows * half, [core, start, new_rows], *small, near, far,
    )


def slope_left(row, logits_ref, info_ref, norm_ref):
    hits = (row == info_ref[0:1, :].astype(I32)).astype(F32)
    return info_ref[2:3, :] * (jnp.exp(logits_ref[...] - norm_ref[...]) - hits)


def onehot_left(row, info_ref):
    return (row == info_ref[1:2, :].astype(I32)).astype(F32)


def local(hidden, targets, token_weight, head_weight, token_ids, embed_cotangent, new_rows):
    core = lax.axis_index("c")
    chips = lax.axis_size("y") * lax.axis_size("x") * lax.axis_size("z")
    devices = 2 * chips
    voc_rows = head_weight.shape[0]
    device = ((lax.axis_index("y") * lax.axis_size("x") + lax.axis_index("x"))
              * lax.axis_size("z") + lax.axis_index("z")) * 2 + core
    at_core = core[None].astype(I32)
    at_device = device[None].astype(I32)
    start = at_device * voc_rows

    mine, theirs = own_block(
        at_core, targets, token_weight.astype(F32), token_ids, hidden, embed_cotangent)
    blocks = chip_blocks(at_core, chips, mine, swap_cores(theirs))
    gathered = lax.all_to_all(blocks, CHIPS, 0, 0, tiled=True)
    near, near_cotangent, info = token_rows(gathered)
    far = swap_cores(near)
    partial, table = near_logits(at_core, near, head_weight)
    logits, stats, left, away = far_logits(at_core, start, devices, partial, info, far, table)

    stats = lax.all_to_all(stats, ALL, 0, 0, tiled=True)
    away = swap_cores(away)
    home = feature_partials(at_core, left, head_weight)
    far_cotangent = swap_cores(near_cotangent)

    pair, norm, loss = scaled_pair(at_device, stats, info, home, away)
    grad_hidden = summed_parts(lax.all_to_all(pair, CHIPS, 0, 0, tiled=True))

    grad_head = row_gradient(
        "grad_head", slope_left, at_core, start, new_rows, voc_rows, [logits, info, norm], near, far)
    grad_embed = row_gradient(
        "grad_embed", onehot_left, at_core, start, new_rows, voc_rows, [info], near_cotangent, far_cotangent)
    return (loss[0, 0], grad_hidden, grad_head, grad_embed)


def solution(mesh):
    grid = Mesh(mesh.devices.reshape(4, 4, 4, 2), ALL)
    rows = P(ALL)
    in_specs = (P(ALL, None), rows, rows, P(ALL, None), rows, P(ALL, None), P())
    out_specs = (P(), P("y", ("x", "z", "c")), P(ALL, None), P(ALL, None))
    return jax.shard_map(local, mesh=grid, in_specs=in_specs, out_specs=out_specs, check_vma=False)
```

```python
import jax
import jax.numpy as jnp
from jax import lax
from jax.experimental import pallas as pl
from jax.experimental.pallas import tpu as pltpu
from jax.sharding import Mesh, PartitionSpec as P

CHIPS = ("y", "x", "z")
ALL = ("y", "x", "z", "c")
LANES = 128
VMEM_LIMIT = 24 * 1024 * 1024
F32, BF16, I32 = jnp.float32, jnp.bfloat16, jnp.int32
NT = (((1,), (1,)), ((), ()))
WHOLE = pl.BlockSpec(memory_space=pltpu.VMEM)
IN_HBM = pl.BlockSpec(memory_space=pltpu.HBM)


def call(kernel, name, out_shape, grid, in_specs, out_specs, scratch, flops, moved, scalars, *arrays):
    return pl.pallas_call(
        kernel,
        name=name,
        out_shape=out_shape,
        grid_spec=pltpu.PrefetchScalarGridSpec(
            num_scalar_prefetch=len(scalars),
            grid=grid,
            in_specs=in_specs,
            out_specs=out_specs,
            scratch_shapes=scratch,
        ),
        compiler_params=pltpu.CompilerParams(vmem_limit_bytes=VMEM_LIMIT),
        cost_estimate=pl.CostEstimate(flops=flops, bytes_accessed=moved, transcendentals=0),
    )(*scalars, *arrays)


def in_hbm(value):
    return pltpu.with_memory_space_constraint(value, pltpu.HBM)


def swap_cores(value):
    return lax.ppermute(value, "c", [(0, 1), (1, 0)])


def quarters_around(value):
    count = lax.axis_size("x") * lax.axis_size("z")
    bits = [0, 1, lax.axis_size("z"), lax.axis_size("z") + 1]
    return [value] + [
        lax.ppermute(value, ("x", "z"), [(i, i ^ bit) for i in range(count)]) for bit in bits[1:]]


def device_blocks(targets, weights, ids, hidden, cotangent, sizes):
    held, width = hidden.shape
    half, quarter = width // 2, width // 8
    kept = half + LANES
    devices = 2 * sizes[0] * sizes[1] * sizes[2]

    def kernel(targets_hbm, weights_hbm, ids_hbm, hidden_hbm, cotangent_hbm, out_ref,
               targets_ref, weights_ref, ids_ref, hidden_ref, cotangent_ref, sems):
        pairs = [(targets_hbm, targets_ref), (ids_hbm, ids_ref), (weights_hbm, weights_ref),
                 (hidden_hbm, hidden_ref), (cotangent_hbm, cotangent_ref)]
        copies = [pltpu.make_async_copy(source, target, sems.at[place])
                  for place, (source, target) in enumerate(pairs)]
        for copy in copies:
            copy.start()
        for copy in copies:
            copy.wait()
        row = lax.broadcasted_iota(I32, (held, LANES), 0)
        lane = lax.broadcasted_iota(I32, (held, LANES), 1)
        meta = jnp.zeros((held, LANES), F32)
        for token in range(held):
            target, name = targets_ref[token], ids_ref[token]
            values = [(target >> 12) & 63, (target >> 6) & 63, target & 63,
                      (name >> 12) & 63, (name >> 6) & 63, name & 63]
            values = [value.astype(F32) for value in values]
            for place, value in enumerate(values):
                meta = jnp.where((row == token) & (lane == place), value, meta)
        weights = weights_ref[...].astype(F32).reshape(held, 1)
        meta = jnp.where(lane == 6, weights, meta).astype(BF16)
        kinds = [
            jnp.concatenate([
                hidden_ref[:, core * half:(core + 1) * half], meta,
                cotangent_ref[:, core * half + part * quarter:core * half + (part + 1) * quarter]], axis=1)
            for part in range(4) for core in range(2)]
        for device in range(devices):
            core, z, x = device % 2, device // 2 % sizes[2], device // 2 // sizes[2] % sizes[1]
            out_ref[device] = kinds[(x % 2 * 2 + z % 2) * 2 + core]

    return call(
        kernel, "device_blocks", jax.ShapeDtypeStruct((devices, held, kept + quarter), BF16), (),
        [IN_HBM] * 5, WHOLE,
        [
            pltpu.SMEM((held,), I32), pltpu.VMEM((held,), BF16), pltpu.SMEM((held,), I32),
            pltpu.VMEM((held, width), BF16), pltpu.VMEM((held, width), BF16),
            pltpu.SemaphoreType.DMA((5,)),
        ],
        0, 4 * devices * held * half, [], in_hbm(targets), in_hbm(weights), in_hbm(ids), in_hbm(hidden),
        in_hbm(cotangent),
    )


def token_rows(gathered, half):
    chips, held, _ = gathered.shape
    tokens, kept, quarter = chips * held, half + LANES, half // 4

    def kernel(gathered_ref, hidden_ref, quarter_ref, info_ref):
        hidden_ref[...] = gathered_ref[:, :, :half].reshape(tokens, half)
        quarter_ref[...] = gathered_ref[:, :, kept:].reshape(tokens, quarter)
        rows = jnp.transpose(gathered_ref[:, :, half:kept].reshape(tokens, LANES).astype(F32))
        targets = rows[0:1] * 4096.0 + rows[1:2] * 64.0 + rows[2:3]
        ids = rows[3:4] * 4096.0 + rows[4:5] * 64.0 + rows[5:6]
        info_ref[...] = jnp.concatenate([targets, ids, rows[6:7], jnp.zeros((5, tokens), F32)], axis=0)

    return call(
        kernel, "token_rows",
        [jax.ShapeDtypeStruct((tokens, half), BF16), jax.ShapeDtypeStruct((tokens, quarter), BF16),
         jax.ShapeDtypeStruct((8, tokens), F32)],
        (), [WHOLE], [WHOLE] * 3, [], 0, 4 * tokens * half, [], gathered,
    )


def joined_quarters(own, quarters, after):
    tokens, quarter = quarters[0].shape

    def kernel(own_ref, *refs):
        for place, ref in enumerate(refs[:4]):
            first = pl.multiple_of((own_ref[0] ^ place) * quarter, quarter)
            refs[-1][:, pl.ds(first, quarter)] = ref[...]

    return call(
        kernel, "joined_quarters", jax.ShapeDtypeStruct((tokens, 4 * quarter), BF16),
        (), [WHOLE] * 4 + [IN_HBM], WHOLE, [], 0, 16 * tokens * quarter, [own], *quarters, after,
    )


def feature_products(side, left_ref, head_ref, first, blocks):
    count = left_ref.shape[0]
    for block in range(first, first + blocks, 2):
        columns = jnp.concatenate([
            head_ref[:, pl.ds(pl.multiple_of((2 * place + side) * LANES, LANES), LANES)]
            for place in (block, block + 1)], axis=1)
        for line in range(0, count, count // 2):
            lines = slice(line, line + count // 2)
            total = jnp.dot(left_ref[lines, :], columns, preferred_element_type=F32).astype(BF16)
            yield block, lines, total[:, :LANES], total[:, LANES:]


def local_logits(core, start, devices, info, near, far, head_weight):
    tokens = near.shape[0]
    rows, width = head_weight.shape
    half, step = width // 2, 256
    blocks = half // LANES

    def kernel(core_ref, start_ref, info_ref, near_ref, far_ref, head_hbm,
               logits_hbm, stats_hbm, left_hbm, away_hbm, last_ref,
               logits_ref, stats_ref, left_ref, away_ref, head_ref, sems, away_sems, head_sems):
        loads = [
            pltpu.make_async_copy(
                head_hbm.at[pl.ds(place, step)], head_ref.at[pl.ds(place, step)], head_sems.at[place // step])
            for place in range(0, rows, step)]
        for load in loads:
            load.start()
        other = 1 - core_ref[0]
        near_columns = pl.ds(pl.multiple_of(core_ref[0] * half, half), half)
        far_columns = pl.ds(pl.multiple_of(other * half, half), half)
        left_ref[tokens:, :] = (
            lax.broadcasted_iota(I32, (tokens, rows), 1) + start_ref[0]
            == jnp.transpose(info_ref[...])[:, 0:1].astype(I32)).astype(F32).astype(BF16)
        for load, place in zip(loads, range(0, rows, step)):
            load.wait()
            logits_ref[place:place + step, :] = lax.dot_general(
                head_ref[place:place + step, near_columns], near_ref[...], NT, preferred_element_type=F32)
        for place in range(0, rows, step):
            logits_ref[place:place + step, :] += lax.dot_general(
                head_ref[place:place + step, far_columns], far_ref[...], NT, preferred_element_type=F32)
        copies = [pltpu.make_async_copy(logits_ref, logits_hbm, sems.at[0])]
        copies[-1].start()
        logits = logits_ref[...]
        peak = jnp.max(logits, axis=0, keepdims=True)
        powers = jnp.exp(logits - peak)
        total = jnp.sum(powers, axis=0, keepdims=True)
        row = lax.broadcasted_iota(I32, (rows, tokens), 0) + start_ref[0]
        hits = row == info_ref[0:1, :].astype(I32)
        picked = jnp.sum(jnp.where(hits, logits, 0.0), axis=0, keepdims=True)
        last_ref[...] = jnp.concatenate([peak, picked, jnp.zeros((6, tokens), F32)], axis=0)
        local_norm = peak + jnp.log(total)
        loss = jnp.sum(info_ref[2:3, :] * picked, axis=1, keepdims=True)
        block = jnp.concatenate(
            [local_norm[:, place:place + LANES] for place in range(0, tokens, LANES)]
            + [jnp.broadcast_to(loss, (4 - tokens // LANES, LANES))], axis=0)
        stats_ref[...] = jnp.broadcast_to(block[None], stats_ref.shape)
        copies.append(pltpu.make_async_copy(stats_ref, stats_hbm, sems.at[1]))
        copies[-1].start()
        left_ref[:tokens, :] = jnp.transpose(jnp.where(hits, 0.0, powers)).astype(BF16)
        copies.append(pltpu.make_async_copy(left_ref, left_hbm, sems.at[2]))
        copies[-1].start()
        for first in range(0, blocks, 4):
            for block, lines, even, odd in feature_products(other, left_ref, head_ref, first, 4):
                away_ref[block, lines, :] = even
                away_ref[block + 1, lines, :] = odd
            part = pl.ds(first, 4)
            copies.append(pltpu.make_async_copy(away_ref.at[part], away_hbm.at[part], away_sems.at[first // 4]))
            copies[-1].start()
        for copy in copies:
            copy.wait()

    shapes = [
        ((rows, tokens), F32), ((devices, 4, LANES), F32),
        ((2 * tokens, rows), BF16), ((blocks, 2 * tokens, LANES), BF16),
    ]
    return call(
        kernel, "local_logits",
        [pltpu.HBM(*shape) for shape in shapes] + [jax.ShapeDtypeStruct((8, tokens), F32)],
        (), [WHOLE] * 3 + [IN_HBM], [IN_HBM] * 4 + [WHOLE],
        [pltpu.VMEM(*shape) for shape in shapes]
        + [pltpu.VMEM((rows, width), BF16), pltpu.SemaphoreType.DMA((3,)),
           pltpu.SemaphoreType.DMA((blocks // 4,)), pltpu.SemaphoreType.DMA((rows // step,))],
        8 * tokens * rows * half, 4 * rows * half, [core, start], info, near, far, in_hbm(head_weight),
    )


def feature_partials(core, left, head_weight):
    count, rows = left.shape
    width = head_weight.shape[1]
    blocks = width // (2 * LANES)
    step = 1024
    held = step // (2 * LANES)

    def kernel(core_ref, left_ref, head_hbm, out_hbm, head_ref, out_ref, head_sems, out_sems):
        loads = [
            pltpu.make_async_copy(head_hbm.at[:, pl.ds(place * step, step)], head_ref.at[place], head_sems.at[place])
            for place in range(width // step)]
        for load in loads:
            load.start()
        stores = []
        for place, load in enumerate(loads):
            load.wait()
            for block, lines, even, odd in feature_products(core_ref[0], left_ref, head_ref.at[place], 0, held):
                out_ref[place * held + block, lines, :] = even
                out_ref[place * held + block + 1, lines, :] = odd
            part = pl.ds(place * held, held)
            stores.append(pltpu.make_async_copy(out_ref.at[part], out_hbm.at[part], out_sems.at[place]))
            stores[-1].start()
        for store in stores:
            store.wait()

    shape = ((blocks, count, LANES), BF16)
    return call(
        kernel, "feature_partials", pltpu.HBM(*shape), (), [WHOLE, IN_HBM], IN_HBM,
        [
            pltpu.VMEM((width // step, rows, step), BF16), pltpu.VMEM(*shape),
            pltpu.SemaphoreType.DMA((width // step,)), pltpu.SemaphoreType.DMA((width // step,)),
        ],
        1 << 35, 2 * rows * width, [core], left, in_hbm(head_weight),
    )


def scaled_pair(stats, info, last, other_last, home, away):
    tokens = info.shape[1]
    blocks = home.shape[0]
    sections = lax.axis_size("y")
    owned = tokens // sections
    lines = tokens // LANES

    def kernel(stats_ref, info_ref, last_ref, other_last_ref, home_hbm, away_hbm, out_hbm, norm_ref, loss_ref,
               home_ref, away_ref, out_ref, in_sems, out_sems):
        loads = []
        for section in range(sections):
            power = pl.ds(section * owned, owned)
            hit = pl.ds(tokens + section * owned, owned)
            loads.append([
                pltpu.make_async_copy(source.at[:, part, :], target.at[:, part, :], in_sems.at[section, place])
                for place, (source, target, part) in enumerate([
                    (home_hbm, home_ref, power), (away_hbm, away_ref, power),
                    (home_hbm, home_ref, hit), (away_hbm, away_ref, hit)])])
            for load in loads[-1]:
                load.start()

        def flat(block, first):
            return jnp.concatenate([block[first + line:first + line + 1] for line in range(lines)], axis=1)

        everyone = stats_ref[...]
        peaks = jnp.max(everyone, axis=0)
        totals = jnp.sum(jnp.exp(everyone - peaks[None]), axis=0)
        norm = flat(peaks, 0) + jnp.log(flat(totals, 0))
        weights = info_ref[2:3, :]
        norm_ref[...] = norm
        picked = jnp.sum(everyone, axis=0)[lines:lines + 1, 0:1]
        loss_ref[...] = ((jnp.sum(weights * norm, axis=1, keepdims=True) - picked)
                         / jnp.sum(weights, axis=1, keepdims=True))
        target = jnp.minimum(last_ref[1:2, :] + other_last_ref[1:2, :], norm)
        scale = jnp.transpose(jnp.concatenate([
            weights * jnp.exp(last_ref[0:1, :] - norm),
            weights * jnp.exp(other_last_ref[0:1, :] - norm),
            weights * (jnp.exp(target - norm) - 1.0),
            jnp.zeros((5, tokens), F32),
        ], axis=0))
        stores = []
        for section in range(sections):
            for load in loads[section]:
                load.wait()
            power = slice(section * owned, (section + 1) * owned)
            hit = slice(tokens + section * owned, tokens + (section + 1) * owned)
            one, two, three = (
                jnp.broadcast_to(scale[power, place:place + 1], (owned, LANES)) for place in range(3))
            for block in range(blocks):
                value = home_ref[block, power, :].astype(F32) * one + away_ref[block, power, :].astype(F32) * two
                hits = (home_ref[block, hit, :] + away_ref[block, hit, :]).astype(F32)
                out_ref[section * blocks + block] = (value + hits * three).astype(BF16)
            part = pl.ds(section * blocks, blocks)
            stores.append(pltpu.make_async_copy(out_ref.at[part], out_hbm.at[part], out_sems.at[section]))
            stores[-1].start()
        for store in stores:
            store.wait()

    return call(
        kernel, "scaled_pair",
        [
            pltpu.HBM((sections * blocks, owned, LANES), BF16),
            jax.ShapeDtypeStruct((1, tokens), F32),
            jax.ShapeDtypeStruct((1, 1), F32),
        ],
        (), [WHOLE] * 4 + [IN_HBM] * 2, [IN_HBM, WHOLE, WHOLE],
        [
            pltpu.VMEM(home.shape, BF16), pltpu.VMEM(away.shape, BF16),
            pltpu.VMEM((sections * blocks, owned, LANES), BF16),
            pltpu.SemaphoreType.DMA((sections, 4)), pltpu.SemaphoreType.DMA((sections,)),
        ],
        10 * tokens * blocks * LANES, 10 * tokens * blocks * LANES, [],
        stats, info, last, other_last, in_hbm(home), in_hbm(away),
    )


def summed_parts(parts):
    count, rows, width = parts.shape

    def kernel(parts_ref, out_ref):
        out_ref[...] = jnp.sum(parts_ref[...].astype(F32), axis=0).astype(BF16)

    return call(
        kernel, "summed_parts", jax.ShapeDtypeStruct((rows, width), BF16), (), [WHOLE], WHOLE,
        [], count * rows * width, 2 * count * rows * width, [], parts,
    )


def row_gradient(name, make_left, core, start, new_rows, rows, small, near, far, step=1024):
    tokens = near.shape[0]
    half = near.shape[1]
    steps = half // step

    def kernel(core_ref, start_ref, ranges_ref, *refs):
        small_refs, (near_ref, far_ref, out_ref, left_ref) = refs[:len(small)], refs[len(small):]
        index = pl.program_id(0)

        @pl.when(index == 0)
        def _():
            lane_row = lax.broadcasted_iota(I32, (8, rows), 1) + start_ref[0]
            inside = jnp.zeros((8, rows), F32)
            for place in range(new_rows.shape[0]):
                within = (lane_row >= ranges_ref[place, 0]) & (lane_row < ranges_ref[place, 1])
                inside = jnp.where(within, 1.0, inside)
            gate = jnp.transpose(inside)[:, 0:1]
            row = lax.broadcasted_iota(I32, (rows, tokens), 0) + start_ref[0]
            left_ref[...] = jnp.where(gate > 0.0, make_left(row, *small_refs), 0.0).astype(BF16)

        @pl.when(index < steps)
        def _():
            out_ref[...] = jnp.dot(left_ref[...], near_ref[...], preferred_element_type=F32).astype(BF16)

        @pl.when(index >= steps)
        def _():
            out_ref[...] = jnp.dot(left_ref[...], far_ref[...], preferred_element_type=F32).astype(BF16)

    def out_index(i, core, start, ranges):
        is_far = (i >= steps).astype(I32)
        side = core[0] + is_far - 2 * core[0] * is_far
        return (0, side * steps + i - is_far * steps)

    return call(
        kernel, name,
        jax.ShapeDtypeStruct((rows, 2 * half), BF16),
        (2 * steps,),
        [pl.BlockSpec(array.shape, lambda i, core, start, ranges: (0, 0)) for array in small] + [
            pl.BlockSpec((tokens, step), lambda i, core, start, ranges: (0, jnp.minimum(i, steps - 1))),
            pl.BlockSpec((tokens, step), lambda i, core, start, ranges: (0, jnp.maximum(i - steps, 0))),
        ],
        pl.BlockSpec((rows, step), out_index),
        [pltpu.VMEM((rows, tokens), BF16)],
        4 * rows * tokens * half, 4 * rows * half, [core, start, new_rows], *small, near, far,
    )


def slope_left(row, logits_ref, info_ref, norm_ref):
    hits = (row == info_ref[0:1, :].astype(I32)).astype(F32)
    return info_ref[2:3, :] * (jnp.exp(logits_ref[...] - norm_ref[...]) - hits)


def onehot_left(row, info_ref):
    return (row == info_ref[1:2, :].astype(I32)).astype(F32)


def local(hidden, targets, token_weight, head_weight, token_ids, embed_cotangent, new_rows):
    core = lax.axis_index("c")
    chips = lax.axis_size("y") * lax.axis_size("x") * lax.axis_size("z")
    devices = 2 * chips
    voc_rows = head_weight.shape[0]
    device = ((lax.axis_index("y") * lax.axis_size("x") + lax.axis_index("x"))
              * lax.axis_size("z") + lax.axis_index("z")) * 2 + core
    at_core = core[None].astype(I32)
    start = device[None].astype(I32) * voc_rows

    sizes = tuple(lax.axis_size(name) for name in CHIPS)
    blocks = device_blocks(targets, token_weight, token_ids, hidden, embed_cotangent, sizes)
    gathered = lax.all_to_all(blocks, ALL, 0, 0, tiled=True)
    near, quarter, info = token_rows(gathered, hidden.shape[1] // 2)
    far = swap_cores(near)
    logits, stats, left, away, last = local_logits(at_core, start, devices, info, near, far, head_weight)

    stats = lax.all_to_all(stats, ALL, 0, 0, tiled=True)
    away = swap_cores(away)
    home = feature_partials(at_core, left, head_weight)
    own_quarter = (lax.axis_index("x") % 2 * 2 + lax.axis_index("z") % 2)[None].astype(I32)
    near_cotangent = joined_quarters(own_quarter, quarters_around(quarter), last)
    far_cotangent = swap_cores(near_cotangent)

    pair, norm, loss = scaled_pair(stats, info, last, swap_cores(last), home, away)
    grad_hidden = summed_parts(lax.all_to_all(pair, CHIPS, 0, 0, tiled=True))

    grad_head = row_gradient(
        "grad_head", slope_left, at_core, start, new_rows, voc_rows, [logits, info, norm], near, far)
    grad_embed = row_gradient(
        "grad_embed", onehot_left, at_core, start, new_rows, voc_rows, [info], near_cotangent, far_cotangent)
    return (loss[0, 0], grad_hidden, grad_head, grad_embed)


def solution(mesh):
    grid = Mesh(mesh.devices.reshape(4, 4, 4, 2), ALL)
    rows = P(ALL)
    in_specs = (P(ALL, None), rows, rows, P(ALL, None), rows, P(ALL, None), P())
    out_specs = (P(), P("y", ("x", "z", "c")), P(ALL, None), P(ALL, None))
    return jax.shard_map(local, mesh=grid, in_specs=in_specs, out_specs=out_specs, check_vma=False)
```

```python
import jax
import jax.numpy as jnp
from jax import lax
from jax.experimental import pallas as pl
from jax.experimental.pallas import tpu as pltpu
from jax.sharding import Mesh, PartitionSpec as P

CHIPS = ("y", "x", "z")
ALL = ("y", "x", "z", "c")
LANES = 128
VMEM_LIMIT = 24 * 1024 * 1024
F32, BF16, I32 = jnp.float32, jnp.bfloat16, jnp.int32
NT = (((1,), (1,)), ((), ()))
WHOLE = pl.BlockSpec(memory_space=pltpu.VMEM)
IN_HBM = pl.BlockSpec(memory_space=pltpu.HBM)


def call(kernel, name, out_shape, grid, in_specs, out_specs, scratch, flops, moved, scalars, *arrays):
    return pl.pallas_call(
        kernel,
        name=name,
        out_shape=out_shape,
        grid_spec=pltpu.PrefetchScalarGridSpec(
            num_scalar_prefetch=len(scalars),
            grid=grid,
            in_specs=in_specs,
            out_specs=out_specs,
            scratch_shapes=scratch,
        ),
        compiler_params=pltpu.CompilerParams(vmem_limit_bytes=VMEM_LIMIT),
        cost_estimate=pl.CostEstimate(flops=flops, bytes_accessed=moved, transcendentals=0),
    )(*scalars, *arrays)


def in_hbm(value):
    return pltpu.with_memory_space_constraint(value, pltpu.HBM)


def swap_cores(value):
    return lax.ppermute(value, "c", [(0, 1), (1, 0)])


def quarters_around(value):
    count = lax.axis_size("x") * lax.axis_size("z")
    bits = [0, 1, lax.axis_size("z"), lax.axis_size("z") + 1]
    return [value] + [
        lax.ppermute(value, ("x", "z"), [(i, i ^ bit) for i in range(count)]) for bit in bits[1:]]


def device_blocks(places, targets, weights, ids, hidden, cotangent, sizes):
    held, width = hidden.shape
    half, quarter = width // 2, width // 8
    kept = half + LANES
    devices = 2 * sizes[0] * sizes[1] * sizes[2]

    def kernel(core_ref, start_ref, quarter_ref, targets_hbm, weights_hbm, ids_hbm, hidden_hbm, cotangent_hbm, out_ref,
               targets_ref, weights_ref, ids_ref, hidden_ref, cotangent_ref, sems):
        pairs = [(targets_hbm, targets_ref), (ids_hbm, ids_ref), (weights_hbm, weights_ref),
                 (hidden_hbm, hidden_ref), (cotangent_hbm, cotangent_ref)]
        copies = [pltpu.make_async_copy(source, target, sems.at[place])
                  for place, (source, target) in enumerate(pairs)]
        for copy in copies:
            copy.start()
        for copy in copies:
            copy.wait()
        row = lax.broadcasted_iota(I32, (held, LANES), 0)
        lane = lax.broadcasted_iota(I32, (held, LANES), 1)
        meta = jnp.zeros((held, LANES), F32)
        for token in range(held):
            target, name = targets_ref[token], ids_ref[token]
            values = [(target >> 12) & 63, (target >> 6) & 63, target & 63,
                      (name >> 12) & 63, (name >> 6) & 63, name & 63]
            values = [value.astype(F32) for value in values]
            for place, value in enumerate(values):
                meta = jnp.where((row == token) & (lane == place), value, meta)
        weights = weights_ref[...].astype(F32).reshape(held, 1)
        meta = jnp.where(lane == 6, weights, meta).astype(BF16)
        kinds = [
            jnp.concatenate([
                hidden_ref[:, core * half:(core + 1) * half], meta,
                cotangent_ref[:, core * half + part * quarter:core * half + (part + 1) * quarter]], axis=1)
            for part in range(4) for core in range(2)]
        for device in range(devices):
            core, z, x = device % 2, device // 2 % sizes[2], device // 2 // sizes[2] % sizes[1]
            out_ref[device] = kinds[(x % 2 * 2 + z % 2) * 2 + core]

    return call(
        kernel, "device_blocks", jax.ShapeDtypeStruct((devices, held, kept + quarter), BF16), (),
        [IN_HBM] * 5, WHOLE,
        [
            pltpu.SMEM((held,), I32), pltpu.VMEM((held,), BF16), pltpu.SMEM((held,), I32),
            pltpu.VMEM((held, width), BF16), pltpu.VMEM((held, width), BF16),
            pltpu.SemaphoreType.DMA((5,)),
        ],
        0, 4 * devices * held * half, places, in_hbm(targets), in_hbm(weights), in_hbm(ids), in_hbm(hidden),
        in_hbm(cotangent),
    )


def token_rows(gathered, half):
    chips, held, _ = gathered.shape
    tokens, kept, quarter = chips * held, half + LANES, half // 4

    def kernel(gathered_ref, hidden_ref, quarter_ref, info_ref):
        hidden_ref[...] = gathered_ref[:, :, :half].reshape(tokens, half)
        quarter_ref[...] = gathered_ref[:, :, kept:].reshape(tokens, quarter)
        rows = jnp.transpose(gathered_ref[:, :, half:kept].reshape(tokens, LANES).astype(F32))
        targets = rows[0:1] * 4096.0 + rows[1:2] * 64.0 + rows[2:3]
        ids = rows[3:4] * 4096.0 + rows[4:5] * 64.0 + rows[5:6]
        info_ref[...] = jnp.concatenate([targets, ids, rows[6:7], jnp.zeros((5, tokens), F32)], axis=0)

    return call(
        kernel, "token_rows",
        [jax.ShapeDtypeStruct((tokens, half), BF16), jax.ShapeDtypeStruct((tokens, quarter), BF16),
         jax.ShapeDtypeStruct((8, tokens), F32)],
        (), [WHOLE], [WHOLE] * 3, [], 1 << 33, 4 * tokens * half, [], gathered,
    )


def joined_quarters(own, quarters, after):
    tokens, quarter = quarters[0].shape

    def kernel(own_ref, *refs):
        for place, ref in enumerate(refs[:4]):
            first = pl.multiple_of((own_ref[0] ^ place) * quarter, quarter)
            refs[-1][:, pl.ds(first, quarter)] = ref[...]

    return call(
        kernel, "joined_quarters", jax.ShapeDtypeStruct((tokens, 4 * quarter), BF16),
        (), [WHOLE] * 4 + [IN_HBM], WHOLE, [], 0, 16 * tokens * quarter, [own], *quarters, after,
    )


def feature_products(side, left_ref, head_ref, first, blocks):
    count = left_ref.shape[0]
    for block in range(first, first + blocks, 2):
        columns = jnp.concatenate([
            head_ref[:, pl.ds(pl.multiple_of((2 * place + side) * LANES, LANES), LANES)]
            for place in (block, block + 1)], axis=1)
        for line in range(0, count, count // 2):
            lines = slice(line, line + count // 2)
            total = jnp.dot(left_ref[lines, :], columns, preferred_element_type=F32).astype(BF16)
            yield block, lines, total[:, :LANES], total[:, LANES:]


def local_logits(core, start, devices, info, near, far, head_weight):
    tokens = near.shape[0]
    rows, width = head_weight.shape
    half, step = width // 2, 256
    blocks = half // LANES

    def kernel(core_ref, start_ref, info_ref, near_ref, far_ref, head_ref,
               logits_hbm, stats_hbm, left_hbm, away_hbm, last_ref,
               logits_ref, stats_ref, left_ref, away_ref, sems, away_sems):
        other = 1 - core_ref[0]
        near_columns = pl.ds(pl.multiple_of(core_ref[0] * half, half), half)
        far_columns = pl.ds(pl.multiple_of(other * half, half), half)
        left_ref[tokens:, :] = (
            lax.broadcasted_iota(I32, (tokens, rows), 1) + start_ref[0]
            == jnp.transpose(info_ref[...])[:, 0:1].astype(I32)).astype(F32).astype(BF16)
        for place in range(0, rows, step):
            logits_ref[place:place + step, :] = lax.dot_general(
                head_ref[place:place + step, near_columns], near_ref[...], NT, preferred_element_type=F32)
        for place in range(0, rows, step):
            logits_ref[place:place + step, :] += lax.dot_general(
                head_ref[place:place + step, far_columns], far_ref[...], NT, preferred_element_type=F32)
        copies = [pltpu.make_async_copy(logits_ref, logits_hbm, sems.at[0])]
        copies[-1].start()
        logits = logits_ref[...]
        peak = jnp.max(logits, axis=0, keepdims=True)
        powers = jnp.exp(logits - peak)
        total = jnp.sum(powers, axis=0, keepdims=True)
        row = lax.broadcasted_iota(I32, (rows, tokens), 0) + start_ref[0]
        hits = row == info_ref[0:1, :].astype(I32)
        picked = jnp.sum(jnp.where(hits, logits, 0.0), axis=0, keepdims=True)
        last_ref[...] = jnp.concatenate([peak, picked, jnp.zeros((6, tokens), F32)], axis=0)
        local_norm = peak + jnp.log(total)
        loss = jnp.sum(info_ref[2:3, :] * picked, axis=1, keepdims=True)
        block = jnp.concatenate(
            [local_norm[:, place:place + LANES] for place in range(0, tokens, LANES)]
            + [jnp.broadcast_to(loss, (4 - tokens // LANES, LANES))], axis=0)
        stats_ref[...] = jnp.broadcast_to(block[None], stats_ref.shape)
        copies.append(pltpu.make_async_copy(stats_ref, stats_hbm, sems.at[1]))
        copies[-1].start()
        left_ref[:tokens, :] = jnp.transpose(jnp.where(hits, 0.0, powers)).astype(BF16)
        copies.append(pltpu.make_async_copy(left_ref, left_hbm, sems.at[2]))
        copies[-1].start()
        for first in range(0, blocks, 4):
            for block, lines, even, odd in feature_products(other, left_ref, head_ref, first, 4):
                away_ref[block, lines, :] = even
                away_ref[block + 1, lines, :] = odd
            part = pl.ds(first, 4)
            copies.append(pltpu.make_async_copy(away_ref.at[part], away_hbm.at[part], away_sems.at[first // 4]))
            copies[-1].start()
        for copy in copies:
            copy.wait()

    shapes = [
        ((rows, tokens), F32), ((devices, 4, LANES), F32),
        ((2 * tokens, rows), BF16), ((blocks, 2 * tokens, LANES), BF16),
    ]
    return call(
        kernel, "local_logits",
        [pltpu.HBM(*shape) for shape in shapes] + [jax.ShapeDtypeStruct((8, tokens), F32)],
        (), [WHOLE] * 4, [IN_HBM] * 4 + [WHOLE],
        [pltpu.VMEM(*shape) for shape in shapes]
        + [pltpu.SemaphoreType.DMA((3,)), pltpu.SemaphoreType.DMA((blocks // 4,))],
        8 * tokens * rows * half, 4 * rows * half, [core, start], info, near, far, head_weight,
    )


def feature_partials(core, left, head_weight):
    count, rows = left.shape
    width = head_weight.shape[1]
    blocks = width // (2 * LANES)
    step = 1024
    held = step // (2 * LANES)

    def kernel(core_ref, left_ref, head_hbm, out_hbm, head_ref, out_ref, head_sems, out_sems):
        loads = [
            pltpu.make_async_copy(head_hbm.at[:, pl.ds(place * step, step)], head_ref.at[place], head_sems.at[place])
            for place in range(width // step)]
        for load in loads:
            load.start()
        stores = []
        for place, load in enumerate(loads):
            load.wait()
            for block, lines, even, odd in feature_products(core_ref[0], left_ref, head_ref.at[place], 0, held):
                out_ref[place * held + block, lines, :] = even
                out_ref[place * held + block + 1, lines, :] = odd
            part = pl.ds(place * held, held)
            stores.append(pltpu.make_async_copy(out_ref.at[part], out_hbm.at[part], out_sems.at[place]))
            stores[-1].start()
        for store in stores:
            store.wait()

    shape = ((blocks, count, LANES), BF16)
    return call(
        kernel, "feature_partials", pltpu.HBM(*shape), (), [WHOLE, IN_HBM], IN_HBM,
        [
            pltpu.VMEM((width // step, rows, step), BF16), pltpu.VMEM(*shape),
            pltpu.SemaphoreType.DMA((width // step,)), pltpu.SemaphoreType.DMA((width // step,)),
        ],
        1 << 35, 2 * rows * width, [core], left, in_hbm(head_weight),
    )


def scaled_pair(stats, info, last, other_last, home, away):
    tokens = info.shape[1]
    blocks = home.shape[0]
    sections = lax.axis_size("y")
    owned = tokens // sections
    lines = tokens // LANES

    def kernel(stats_ref, info_ref, last_ref, other_last_ref, home_hbm, away_hbm, out_hbm, norm_ref, loss_ref,
               home_ref, away_ref, out_ref, in_sems, out_sems):
        loads = []
        for section in range(sections):
            power = pl.ds(section * owned, owned)
            hit = pl.ds(tokens + section * owned, owned)
            loads.append([
                pltpu.make_async_copy(source.at[:, part, :], target.at[:, part, :], in_sems.at[section, place])
                for place, (source, target, part) in enumerate([
                    (home_hbm, home_ref, power), (away_hbm, away_ref, power),
                    (home_hbm, home_ref, hit), (away_hbm, away_ref, hit)])])
            for load in loads[-1]:
                load.start()

        def flat(block, first):
            return jnp.concatenate([block[first + line:first + line + 1] for line in range(lines)], axis=1)

        everyone = stats_ref[...]
        peaks = jnp.max(everyone, axis=0)
        totals = jnp.sum(jnp.exp(everyone - peaks[None]), axis=0)
        norm = flat(peaks, 0) + jnp.log(flat(totals, 0))
        weights = info_ref[2:3, :]
        norm_ref[...] = norm
        picked = jnp.sum(everyone, axis=0)[lines:lines + 1, 0:1]
        loss_ref[...] = ((jnp.sum(weights * norm, axis=1, keepdims=True) - picked)
                         / jnp.sum(weights, axis=1, keepdims=True))
        target = jnp.minimum(last_ref[1:2, :] + other_last_ref[1:2, :], norm)
        scale = jnp.transpose(jnp.concatenate([
            weights * jnp.exp(last_ref[0:1, :] - norm),
            weights * jnp.exp(other_last_ref[0:1, :] - norm),
            weights * (jnp.exp(target - norm) - 1.0),
            jnp.zeros((5, tokens), F32),
        ], axis=0))
        stores = []
        for section in range(sections):
            for load in loads[section]:
                load.wait()
            power = slice(section * owned, (section + 1) * owned)
            hit = slice(tokens + section * owned, tokens + (section + 1) * owned)
            one, two, three = (
                jnp.broadcast_to(scale[power, place:place + 1], (owned, LANES)) for place in range(3))
            for block in range(blocks):
                value = home_ref[block, power, :].astype(F32) * one + away_ref[block, power, :].astype(F32) * two
                hits = (home_ref[block, hit, :] + away_ref[block, hit, :]).astype(F32)
                out_ref[section * blocks + block] = (value + hits * three).astype(BF16)
            part = pl.ds(section * blocks, blocks)
            stores.append(pltpu.make_async_copy(out_ref.at[part], out_hbm.at[part], out_sems.at[section]))
            stores[-1].start()
        for store in stores:
            store.wait()

    return call(
        kernel, "scaled_pair",
        [
            pltpu.HBM((sections * blocks, owned, LANES), BF16),
            jax.ShapeDtypeStruct((1, tokens), F32),
            jax.ShapeDtypeStruct((1, 1), F32),
        ],
        (), [WHOLE] * 4 + [IN_HBM] * 2, [IN_HBM, WHOLE, WHOLE],
        [
            pltpu.VMEM(home.shape, BF16), pltpu.VMEM(away.shape, BF16),
            pltpu.VMEM((sections * blocks, owned, LANES), BF16),
            pltpu.SemaphoreType.DMA((sections, 4)), pltpu.SemaphoreType.DMA((sections,)),
        ],
        10 * tokens * blocks * LANES, 10 * tokens * blocks * LANES, [],
        stats, info, last, other_last, in_hbm(home), in_hbm(away),
    )


def summed_parts(parts):
    count, rows, width = parts.shape

    def kernel(parts_ref, out_ref):
        out_ref[...] = jnp.sum(parts_ref[...].astype(F32), axis=0).astype(BF16)

    return call(
        kernel, "summed_parts", jax.ShapeDtypeStruct((rows, width), BF16), (), [WHOLE], WHOLE,
        [], count * rows * width, 2 * count * rows * width, [], parts,
    )


def row_gradient(name, make_left, core, start, new_rows, rows, small, near, far, step=1024):
    tokens = near.shape[0]
    half = near.shape[1]
    steps = half // step

    def kernel(core_ref, start_ref, ranges_ref, *refs):
        small_refs, (near_ref, far_ref, out_ref, left_ref) = refs[:len(small)], refs[len(small):]
        index = pl.program_id(0)

        @pl.when(index == 0)
        def _():
            lane_row = lax.broadcasted_iota(I32, (8, rows), 1) + start_ref[0]
            inside = jnp.zeros((8, rows), F32)
            for place in range(new_rows.shape[0]):
                within = (lane_row >= ranges_ref[place, 0]) & (lane_row < ranges_ref[place, 1])
                inside = jnp.where(within, 1.0, inside)
            gate = jnp.transpose(inside)[:, 0:1]
            row = lax.broadcasted_iota(I32, (rows, tokens), 0) + start_ref[0]
            left_ref[...] = jnp.where(gate > 0.0, make_left(row, *small_refs), 0.0).astype(BF16)

        @pl.when(index < steps)
        def _():
            out_ref[...] = jnp.dot(left_ref[...], near_ref[...], preferred_element_type=F32).astype(BF16)

        @pl.when(index >= steps)
        def _():
            out_ref[...] = jnp.dot(left_ref[...], far_ref[...], preferred_element_type=F32).astype(BF16)

    def out_index(i, core, start, ranges):
        is_far = (i >= steps).astype(I32)
        side = core[0] + is_far - 2 * core[0] * is_far
        return (0, side * steps + i - is_far * steps)

    return call(
        kernel, name,
        jax.ShapeDtypeStruct((rows, 2 * half), BF16),
        (2 * steps,),
        [pl.BlockSpec(array.shape, lambda i, core, start, ranges: (0, 0)) for array in small] + [
            pl.BlockSpec((tokens, step), lambda i, core, start, ranges: (0, jnp.minimum(i, steps - 1))),
            pl.BlockSpec((tokens, step), lambda i, core, start, ranges: (0, jnp.maximum(i - steps, 0))),
        ],
        pl.BlockSpec((rows, step), out_index),
        [pltpu.VMEM((rows, tokens), BF16)],
        4 * rows * tokens * half, 4 * rows * half, [core, start, new_rows], *small, near, far,
    )


def slope_left(row, logits_ref, info_ref, norm_ref):
    hits = (row == info_ref[0:1, :].astype(I32)).astype(F32)
    return info_ref[2:3, :] * (jnp.exp(logits_ref[...] - norm_ref[...]) - hits)


def onehot_left(row, info_ref):
    return (row == info_ref[1:2, :].astype(I32)).astype(F32)


def local(hidden, targets, token_weight, head_weight, token_ids, embed_cotangent, new_rows):
    core = lax.axis_index("c")
    chips = lax.axis_size("y") * lax.axis_size("x") * lax.axis_size("z")
    devices = 2 * chips
    voc_rows = head_weight.shape[0]
    device = ((lax.axis_index("y") * lax.axis_size("x") + lax.axis_index("x"))
              * lax.axis_size("z") + lax.axis_index("z")) * 2 + core
    at_core = core[None].astype(I32)
    start = device[None].astype(I32) * voc_rows
    own_quarter = (lax.axis_index("x") % 2 * 2 + lax.axis_index("z") % 2)[None].astype(I32)

    sizes = tuple(lax.axis_size(name) for name in CHIPS)
    blocks = device_blocks([at_core, start, own_quarter], targets, token_weight, token_ids, hidden, embed_cotangent, sizes)
    gathered = lax.all_to_all(blocks, ALL, 0, 0, tiled=True)
    near, quarter, info = token_rows(gathered, hidden.shape[1] // 2)
    far = swap_cores(near)
    logits, stats, left, away, last = local_logits(at_core, start, devices, info, near, far, head_weight)

    stats = lax.all_to_all(stats, ALL, 0, 0, tiled=True)
    away = swap_cores(away)
    home = feature_partials(at_core, left, head_weight)
    near_cotangent = joined_quarters(own_quarter, quarters_around(quarter), last)
    far_cotangent = swap_cores(near_cotangent)

    pair, norm, loss = scaled_pair(stats, info, last, swap_cores(last), home, away)
    grad_hidden = summed_parts(lax.all_to_all(pair, CHIPS, 0, 0, tiled=True))

    grad_head = row_gradient(
        "grad_head", slope_left, at_core, start, new_rows, voc_rows, [logits, info, norm], near, far)
    grad_embed = row_gradient(
        "grad_embed", onehot_left, at_core, start, new_rows, voc_rows, [info], near_cotangent, far_cotangent)
    return (loss[0, 0], grad_hidden, grad_head, grad_embed)


def solution(mesh):
    grid = Mesh(mesh.devices.reshape(4, 4, 4, 2), ALL)
    rows = P(ALL)
    in_specs = (P(ALL, None), rows, rows, P(ALL, None), rows, P(ALL, None), P())
    out_specs = (P(), P("y", ("x", "z", "c")), P(ALL, None), P(ALL, None))
    return jax.shard_map(local, mesh=grid, in_specs=in_specs, out_specs=out_specs, check_vma=False)
```

```python
import jax
import jax.numpy as jnp
from jax import lax
from jax.experimental import pallas as pl
from jax.experimental.pallas import tpu as pltpu
from jax.sharding import Mesh, PartitionSpec as P

CHIPS = ("y", "x", "z")
ALL = ("y", "x", "z", "c")
LANES = 128
VMEM_LIMIT = 24 * 1024 * 1024
F32, BF16, I32 = jnp.float32, jnp.bfloat16, jnp.int32
NT = (((1,), (1,)), ((), ()))
WHOLE = pl.BlockSpec(memory_space=pltpu.VMEM)
IN_HBM = pl.BlockSpec(memory_space=pltpu.HBM)


def call(kernel, name, out_shape, grid, in_specs, out_specs, scratch, flops, moved, scalars, *arrays):
    return pl.pallas_call(
        kernel,
        name=name,
        out_shape=out_shape,
        grid_spec=pltpu.PrefetchScalarGridSpec(
            num_scalar_prefetch=len(scalars),
            grid=grid,
            in_specs=in_specs,
            out_specs=out_specs,
            scratch_shapes=scratch,
        ),
        compiler_params=pltpu.CompilerParams(vmem_limit_bytes=VMEM_LIMIT),
        cost_estimate=pl.CostEstimate(flops=flops, bytes_accessed=moved, transcendentals=0),
    )(*scalars, *arrays)


def in_hbm(value):
    return pltpu.with_memory_space_constraint(value, pltpu.HBM)


def swap_cores(value):
    return lax.ppermute(value, "c", [(0, 1), (1, 0)])


def quarters_around(value):
    count = lax.axis_size("x") * lax.axis_size("z")
    bits = [0, 1, lax.axis_size("z"), lax.axis_size("z") + 1]
    return [value] + [
        lax.ppermute(value, ("x", "z"), [(i, i ^ bit) for i in range(count)]) for bit in bits[1:]]


def device_blocks(places, targets, weights, ids, hidden, cotangent, sizes):
    held, width = hidden.shape
    half, quarter = width // 2, width // 8
    kept = half + LANES
    devices = 2 * sizes[0] * sizes[1] * sizes[2]

    def kernel(core_ref, start_ref, quarter_ref, targets_hbm, weights_hbm, ids_hbm, hidden_hbm, cotangent_hbm, out_ref,
               targets_ref, weights_ref, ids_ref, hidden_ref, cotangent_ref, sems):
        pairs = [(targets_hbm, targets_ref), (ids_hbm, ids_ref), (weights_hbm, weights_ref),
                 (hidden_hbm, hidden_ref), (cotangent_hbm, cotangent_ref)]
        copies = [pltpu.make_async_copy(source, target, sems.at[place])
                  for place, (source, target) in enumerate(pairs)]
        for copy in copies:
            copy.start()
        for copy in copies:
            copy.wait()
        row = lax.broadcasted_iota(I32, (held, LANES), 0)
        lane = lax.broadcasted_iota(I32, (held, LANES), 1)
        meta = jnp.zeros((held, LANES), F32)
        for token in range(held):
            target, name = targets_ref[token], ids_ref[token]
            values = [(target >> 12) & 63, (target >> 6) & 63, target & 63,
                      (name >> 12) & 63, (name >> 6) & 63, name & 63]
            values = [value.astype(F32) for value in values]
            for place, value in enumerate(values):
                meta = jnp.where((row == token) & (lane == place), value, meta)
        weights = weights_ref[...].astype(F32).reshape(held, 1)
        meta = jnp.where(lane == 6, weights, meta).astype(BF16)
        kinds = [
            jnp.concatenate([
                hidden_ref[:, core * half:(core + 1) * half], meta,
                cotangent_ref[:, core * half + part * quarter:core * half + (part + 1) * quarter]], axis=1)
            for part in range(4) for core in range(2)]
        for device in range(devices):
            core, z, x = device % 2, device // 2 % sizes[2], device // 2 // sizes[2] % sizes[1]
            out_ref[device] = kinds[(x % 2 * 2 + z % 2) * 2 + core]

    return call(
        kernel, "device_blocks", jax.ShapeDtypeStruct((devices, held, kept + quarter), BF16), (),
        [IN_HBM] * 5, WHOLE,
        [
            pltpu.SMEM((held,), I32), pltpu.VMEM((held,), BF16), pltpu.SMEM((held,), I32),
            pltpu.VMEM((held, width), BF16), pltpu.VMEM((held, width), BF16),
            pltpu.SemaphoreType.DMA((5,)),
        ],
        0, 4 * devices * held * half, places, in_hbm(targets), in_hbm(weights), in_hbm(ids), in_hbm(hidden),
        in_hbm(cotangent),
    )


def token_rows(gathered, half):
    chips, held, _ = gathered.shape
    tokens, kept, quarter = chips * held, half + LANES, half // 4

    def kernel(gathered_ref, hidden_ref, quarter_ref, info_ref):
        hidden_ref[...] = gathered_ref[:, :, :half].reshape(tokens, half)
        quarter_ref[...] = gathered_ref[:, :, kept:].reshape(tokens, quarter)
        rows = jnp.transpose(gathered_ref[:, :, half:kept].reshape(tokens, LANES).astype(F32))
        targets = rows[0:1] * 4096.0 + rows[1:2] * 64.0 + rows[2:3]
        ids = rows[3:4] * 4096.0 + rows[4:5] * 64.0 + rows[5:6]
        info_ref[...] = jnp.concatenate([targets, ids, rows[6:7], jnp.zeros((5, tokens), F32)], axis=0)

    return call(
        kernel, "token_rows",
        [jax.ShapeDtypeStruct((tokens, half), BF16), jax.ShapeDtypeStruct((tokens, quarter), BF16),
         jax.ShapeDtypeStruct((8, tokens), F32)],
        (), [WHOLE], [WHOLE] * 3, [], 1 << 33, 4 * tokens * half, [], gathered,
    )


def joined_quarters(own, quarters, after):
    tokens, quarter = quarters[0].shape

    def kernel(own_ref, *refs):
        for place, ref in enumerate(refs[:4]):
            first = pl.multiple_of((own_ref[0] ^ place) * quarter, quarter)
            refs[-1][:, pl.ds(first, quarter)] = ref[...]

    return call(
        kernel, "joined_quarters", jax.ShapeDtypeStruct((tokens, 4 * quarter), BF16),
        (), [WHOLE] * 4 + [IN_HBM], WHOLE, [], 0, 16 * tokens * quarter, [own], *quarters, after,
    )


def feature_products(side, left_ref, head_ref, first, blocks):
    count = left_ref.shape[0]
    for block in range(first, first + blocks, 2):
        columns = jnp.concatenate([
            head_ref[:, pl.ds(pl.multiple_of((2 * place + side) * LANES, LANES), LANES)]
            for place in (block, block + 1)], axis=1)
        for line in range(0, count, count // 2):
            lines = slice(line, line + count // 2)
            total = jnp.dot(left_ref[lines, :], columns, preferred_element_type=F32).astype(BF16)
            yield block, lines, total[:, :LANES], total[:, LANES:]


def local_logits(core, start, devices, info, near, far, head_weight):
    tokens = near.shape[0]
    rows, width = head_weight.shape
    half, step = width // 2, 256
    blocks = half // LANES

    def kernel(core_ref, start_ref, info_ref, near_ref, far_ref, head_ref,
               logits_hbm, stats_hbm, left_hbm, away_hbm, last_ref,
               logits_ref, stats_ref, left_ref, away_ref, sems, away_sems):
        other = 1 - core_ref[0]
        near_columns = pl.ds(pl.multiple_of(core_ref[0] * half, half), half)
        far_columns = pl.ds(pl.multiple_of(other * half, half), half)
        left_ref[tokens:, :] = (
            lax.broadcasted_iota(I32, (tokens, rows), 1) + start_ref[0]
            == jnp.transpose(info_ref[...])[:, 0:1].astype(I32)).astype(F32).astype(BF16)
        for place in range(0, rows, step):
            logits_ref[place:place + step, :] = lax.dot_general(
                head_ref[place:place + step, near_columns], near_ref[...], NT, preferred_element_type=F32)
        for place in range(0, rows, step):
            logits_ref[place:place + step, :] += lax.dot_general(
                head_ref[place:place + step, far_columns], far_ref[...], NT, preferred_element_type=F32)
        copies = [pltpu.make_async_copy(logits_ref, logits_hbm, sems.at[0])]
        copies[-1].start()
        logits = logits_ref[...]
        peak = jnp.max(logits, axis=0, keepdims=True)
        powers = jnp.exp(logits - peak)
        total = jnp.sum(powers, axis=0, keepdims=True)
        row = lax.broadcasted_iota(I32, (rows, tokens), 0) + start_ref[0]
        hits = row == info_ref[0:1, :].astype(I32)
        picked = jnp.sum(jnp.where(hits, logits, 0.0), axis=0, keepdims=True)
        last_ref[...] = jnp.concatenate([peak, picked, jnp.zeros((6, tokens), F32)], axis=0)
        local_norm = peak + jnp.log(total)
        loss = jnp.sum(info_ref[2:3, :] * picked, axis=1, keepdims=True)
        block = jnp.concatenate([local_norm, jnp.broadcast_to(loss, (1, LANES))], axis=1)
        stats_ref[...] = jnp.broadcast_to(block[None], stats_ref.shape)
        copies.append(pltpu.make_async_copy(stats_ref, stats_hbm, sems.at[1]))
        copies[-1].start()
        left_ref[:tokens, :] = jnp.transpose(jnp.where(hits, 0.0, powers)).astype(BF16)
        copies.append(pltpu.make_async_copy(left_ref, left_hbm, sems.at[2]))
        copies[-1].start()
        for first in range(0, blocks, 4):
            for block, lines, even, odd in feature_products(other, left_ref, head_ref, first, 4):
                away_ref[block, lines, :] = even
                away_ref[block + 1, lines, :] = odd
            part = pl.ds(first, 4)
            copies.append(pltpu.make_async_copy(away_ref.at[part], away_hbm.at[part], away_sems.at[first // 4]))
            copies[-1].start()
        for copy in copies:
            copy.wait()

    shapes = [
        ((rows, tokens), F32), ((devices, 1, tokens + LANES), F32),
        ((2 * tokens, rows), BF16), ((blocks, 2 * tokens, LANES), BF16),
    ]
    return call(
        kernel, "local_logits",
        [pltpu.HBM(*shape) for shape in shapes] + [jax.ShapeDtypeStruct((8, tokens), F32)],
        (), [WHOLE] * 4, [IN_HBM] * 4 + [WHOLE],
        [pltpu.VMEM(*shape) for shape in shapes]
        + [pltpu.SemaphoreType.DMA((3,)), pltpu.SemaphoreType.DMA((blocks // 4,))],
        8 * tokens * rows * half, 4 * rows * half, [core, start], info, near, far, head_weight,
    )


def feature_partials(core, left, head_weight):
    count, rows = left.shape
    width = head_weight.shape[1]
    blocks = width // (2 * LANES)
    step = 1024
    held = step // (2 * LANES)

    def kernel(core_ref, left_ref, head_hbm, out_hbm, head_ref, out_ref, head_sems, out_sems):
        loads = [
            pltpu.make_async_copy(head_hbm.at[:, pl.ds(place * step, step)], head_ref.at[place], head_sems.at[place])
            for place in range(width // step)]
        for load in loads:
            load.start()
        stores = []
        for place, load in enumerate(loads):
            load.wait()
            for block, lines, even, odd in feature_products(core_ref[0], left_ref, head_ref.at[place], 0, held):
                out_ref[place * held + block, lines, :] = even
                out_ref[place * held + block + 1, lines, :] = odd
            part = pl.ds(place * held, held)
            stores.append(pltpu.make_async_copy(out_ref.at[part], out_hbm.at[part], out_sems.at[place]))
            stores[-1].start()
        for store in stores:
            store.wait()

    shape = ((blocks, count, LANES), BF16)
    return call(
        kernel, "feature_partials", pltpu.HBM(*shape), (), [WHOLE, IN_HBM], IN_HBM,
        [
            pltpu.VMEM((width // step, rows, step), BF16), pltpu.VMEM(*shape),
            pltpu.SemaphoreType.DMA((width // step,)), pltpu.SemaphoreType.DMA((width // step,)),
        ],
        1 << 35, 2 * rows * width, [core], left, in_hbm(head_weight),
    )


def scaled_pair(stats, info, last, other_last, home, away):
    tokens = info.shape[1]
    blocks = home.shape[0]
    sections = lax.axis_size("y")
    owned = tokens // sections

    def kernel(stats_ref, info_ref, last_ref, other_last_ref, home_hbm, away_hbm, out_hbm, norm_ref, loss_ref,
               home_ref, away_ref, out_ref, in_sems, out_sems):
        loads = []
        for section in range(sections):
            power = pl.ds(section * owned, owned)
            hit = pl.ds(tokens + section * owned, owned)
            loads.append([
                pltpu.make_async_copy(source.at[:, part, :], target.at[:, part, :], in_sems.at[section, place])
                for place, (source, target, part) in enumerate([
                    (home_hbm, home_ref, power), (away_hbm, away_ref, power),
                    (home_hbm, home_ref, hit), (away_hbm, away_ref, hit)])])
            for load in loads[-1]:
                load.start()

        everyone = stats_ref[:, 0, :]
        norms = everyone[:, :tokens]
        peak = jnp.max(norms, axis=0, keepdims=True)
        norm = peak + jnp.log(jnp.sum(jnp.exp(norms - peak), axis=0, keepdims=True))
        weights = info_ref[2:3, :]
        norm_ref[...] = norm
        picked = jnp.sum(everyone[:, tokens:tokens + 1], axis=0, keepdims=True)
        loss_ref[...] = ((jnp.sum(weights * norm, axis=1, keepdims=True) - picked)
                         / jnp.sum(weights, axis=1, keepdims=True))
        target = jnp.minimum(last_ref[1:2, :] + other_last_ref[1:2, :], norm)
        scale = jnp.transpose(jnp.concatenate([
            weights * jnp.exp(last_ref[0:1, :] - norm),
            weights * jnp.exp(other_last_ref[0:1, :] - norm),
            weights * (jnp.exp(target - norm) - 1.0),
            jnp.zeros((5, tokens), F32),
        ], axis=0))
        stores = []
        for section in range(sections):
            for load in loads[section]:
                load.wait()
            power = slice(section * owned, (section + 1) * owned)
            hit = slice(tokens + section * owned, tokens + (section + 1) * owned)
            one, two, three = (
                jnp.broadcast_to(scale[power, place:place + 1], (owned, LANES)) for place in range(3))
            for block in range(blocks):
                value = home_ref[block, power, :].astype(F32) * one + away_ref[block, power, :].astype(F32) * two
                hits = (home_ref[block, hit, :] + away_ref[block, hit, :]).astype(F32)
                out_ref[section * blocks + block] = (value + hits * three).astype(BF16)
            part = pl.ds(section * blocks, blocks)
            stores.append(pltpu.make_async_copy(out_ref.at[part], out_hbm.at[part], out_sems.at[section]))
            stores[-1].start()
        for store in stores:
            store.wait()

    return call(
        kernel, "scaled_pair",
        [
            pltpu.HBM((sections * blocks, owned, LANES), BF16),
            jax.ShapeDtypeStruct((1, tokens), F32),
            jax.ShapeDtypeStruct((1, 1), F32),
        ],
        (), [WHOLE] * 4 + [IN_HBM] * 2, [IN_HBM, WHOLE, WHOLE],
        [
            pltpu.VMEM(home.shape, BF16), pltpu.VMEM(away.shape, BF16),
            pltpu.VMEM((sections * blocks, owned, LANES), BF16),
            pltpu.SemaphoreType.DMA((sections, 4)), pltpu.SemaphoreType.DMA((sections,)),
        ],
        10 * tokens * blocks * LANES, 10 * tokens * blocks * LANES, [],
        stats, info, last, other_last, in_hbm(home), in_hbm(away),
    )


def summed_parts(parts):
    count, rows, width = parts.shape

    def kernel(parts_ref, out_ref):
        out_ref[...] = jnp.sum(parts_ref[...].astype(F32), axis=0).astype(BF16)

    return call(
        kernel, "summed_parts", jax.ShapeDtypeStruct((rows, width), BF16), (), [WHOLE], WHOLE,
        [], count * rows * width, 2 * count * rows * width, [], parts,
    )


def row_gradient(name, make_left, core, start, new_rows, rows, small, near, far, step=1024):
    tokens = near.shape[0]
    half = near.shape[1]
    steps = half // step

    def kernel(core_ref, start_ref, ranges_ref, *refs):
        small_refs, (near_ref, far_ref, out_ref, left_ref) = refs[:len(small)], refs[len(small):]
        index = pl.program_id(0)

        @pl.when(index == 0)
        def _():
            lane_row = lax.broadcasted_iota(I32, (8, rows), 1) + start_ref[0]
            inside = jnp.zeros((8, rows), F32)
            for place in range(new_rows.shape[0]):
                within = (lane_row >= ranges_ref[place, 0]) & (lane_row < ranges_ref[place, 1])
                inside = jnp.where(within, 1.0, inside)
            gate = jnp.transpose(inside)[:, 0:1]
            row = lax.broadcasted_iota(I32, (rows, tokens), 0) + start_ref[0]
            left_ref[...] = jnp.where(gate > 0.0, make_left(row, *small_refs), 0.0).astype(BF16)

        @pl.when(index < steps)
        def _():
            out_ref[...] = jnp.dot(left_ref[...], near_ref[...], preferred_element_type=F32).astype(BF16)

        @pl.when(index >= steps)
        def _():
            out_ref[...] = jnp.dot(left_ref[...], far_ref[...], preferred_element_type=F32).astype(BF16)

    def out_index(i, core, start, ranges):
        is_far = (i >= steps).astype(I32)
        side = core[0] + is_far - 2 * core[0] * is_far
        return (0, side * steps + i - is_far * steps)

    return call(
        kernel, name,
        jax.ShapeDtypeStruct((rows, 2 * half), BF16),
        (2 * steps,),
        [pl.BlockSpec(array.shape, lambda i, core, start, ranges: (0, 0)) for array in small] + [
            pl.BlockSpec((tokens, step), lambda i, core, start, ranges: (0, jnp.minimum(i, steps - 1))),
            pl.BlockSpec((tokens, step), lambda i, core, start, ranges: (0, jnp.maximum(i - steps, 0))),
        ],
        pl.BlockSpec((rows, step), out_index),
        [pltpu.VMEM((rows, tokens), BF16)],
        4 * rows * tokens * half, 4 * rows * half, [core, start, new_rows], *small, near, far,
    )


def slope_left(row, logits_ref, info_ref, norm_ref):
    hits = (row == info_ref[0:1, :].astype(I32)).astype(F32)
    return info_ref[2:3, :] * (jnp.exp(logits_ref[...] - norm_ref[...]) - hits)


def onehot_left(row, info_ref):
    return (row == info_ref[1:2, :].astype(I32)).astype(F32)


def local(hidden, targets, token_weight, head_weight, token_ids, embed_cotangent, new_rows):
    core = lax.axis_index("c")
    chips = lax.axis_size("y") * lax.axis_size("x") * lax.axis_size("z")
    devices = 2 * chips
    voc_rows = head_weight.shape[0]
    device = ((lax.axis_index("y") * lax.axis_size("x") + lax.axis_index("x"))
              * lax.axis_size("z") + lax.axis_index("z")) * 2 + core
    at_core = core[None].astype(I32)
    start = device[None].astype(I32) * voc_rows
    own_quarter = ((lax.axis_index("x") & 1) * 2 + (lax.axis_index("z") & 1))[None].astype(I32)

    sizes = tuple(lax.axis_size(name) for name in CHIPS)
    blocks = device_blocks([at_core, start, own_quarter], targets, token_weight, token_ids, hidden, embed_cotangent, sizes)
    gathered = lax.all_to_all(blocks, ALL, 0, 0, tiled=True)
    near, quarter, info = token_rows(gathered, hidden.shape[1] // 2)
    far = swap_cores(near)
    logits, stats, left, away, last = local_logits(at_core, start, devices, info, near, far, head_weight)

    stats = lax.all_to_all(stats, ALL, 0, 0, tiled=True)
    away = swap_cores(away)
    home = feature_partials(at_core, left, head_weight)
    near_cotangent = joined_quarters(own_quarter, quarters_around(quarter), last)
    far_cotangent = swap_cores(near_cotangent)

    pair, norm, loss = scaled_pair(stats, info, last, swap_cores(last), home, away)
    grad_hidden = summed_parts(lax.all_to_all(pair, CHIPS, 0, 0, tiled=True))

    grad_head = row_gradient(
        "grad_head", slope_left, at_core, start, new_rows, voc_rows, [logits, info, norm], near, far)
    grad_embed = row_gradient(
        "grad_embed", onehot_left, at_core, start, new_rows, voc_rows, [info], near_cotangent, far_cotangent)
    return (loss[0, 0], grad_hidden, grad_head, grad_embed)


def solution(mesh):
    grid = Mesh(mesh.devices.reshape(4, 4, 4, 2), ALL)
    rows = P(ALL)
    in_specs = (P(ALL, None), rows, rows, P(ALL, None), rows, P(ALL, None), P())
    out_specs = (P(), P("y", ("x", "z", "c")), P(ALL, None), P(ALL, None))
    return jax.shard_map(local, mesh=grid, in_specs=in_specs, out_specs=out_specs, check_vma=False)
```

```python
import jax
import jax.numpy as jnp
from jax import lax
from jax.experimental import pallas as pl
from jax.experimental.pallas import tpu as pltpu
from jax.sharding import Mesh, PartitionSpec as P

CHIPS = ("y", "x", "z")
ALL = ("y", "x", "z", "c")
LANES = 128
VMEM_LIMIT = 24 * 1024 * 1024
F32, BF16, I32 = jnp.float32, jnp.bfloat16, jnp.int32
NT = (((1,), (1,)), ((), ()))
WHOLE = pl.BlockSpec(memory_space=pltpu.VMEM)
IN_HBM = pl.BlockSpec(memory_space=pltpu.HBM)


def call(kernel, name, out_shape, grid, in_specs, out_specs, scratch, flops, moved, scalars, *arrays):
    return pl.pallas_call(
        kernel,
        name=name,
        out_shape=out_shape,
        grid_spec=pltpu.PrefetchScalarGridSpec(
            num_scalar_prefetch=len(scalars),
            grid=grid,
            in_specs=in_specs,
            out_specs=out_specs,
            scratch_shapes=scratch,
        ),
        compiler_params=pltpu.CompilerParams(vmem_limit_bytes=VMEM_LIMIT),
        cost_estimate=pl.CostEstimate(flops=flops, bytes_accessed=moved, transcendentals=0),
    )(*scalars, *arrays)


def in_hbm(value):
    return pltpu.with_memory_space_constraint(value, pltpu.HBM)


def swap_cores(value):
    return lax.ppermute(value, "c", [(0, 1), (1, 0)])


def quarters_around(value):
    count = lax.axis_size("x") * lax.axis_size("z")
    bits = [0, 1, lax.axis_size("z"), lax.axis_size("z") + 1]
    return [value] + [
        lax.ppermute(value, ("x", "z"), [(i, i ^ bit) for i in range(count)]) for bit in bits[1:]]


def device_blocks(places, targets, weights, ids, hidden, cotangent, sizes):
    held, width = hidden.shape
    half, quarter = width // 2, width // 8
    kept = half + LANES
    devices = 2 * sizes[0] * sizes[1] * sizes[2]

    def kernel(core_ref, start_ref, quarter_ref, targets_hbm, weights_hbm, ids_hbm, hidden_hbm, cotangent_hbm, out_ref,
               targets_ref, weights_ref, ids_ref, hidden_ref, cotangent_ref, sems):
        pairs = [(targets_hbm, targets_ref), (ids_hbm, ids_ref), (weights_hbm, weights_ref),
                 (hidden_hbm, hidden_ref), (cotangent_hbm, cotangent_ref)]
        copies = [pltpu.make_async_copy(source, target, sems.at[place])
                  for place, (source, target) in enumerate(pairs)]
        for copy in copies:
            copy.start()
        for copy in copies:
            copy.wait()
        row = lax.broadcasted_iota(I32, (held, LANES), 0)
        lane = lax.broadcasted_iota(I32, (held, LANES), 1)
        meta = jnp.zeros((held, LANES), F32)
        for token in range(held):
            target, name = targets_ref[token], ids_ref[token]
            values = [(target >> 12) & 63, (target >> 6) & 63, target & 63,
                      (name >> 12) & 63, (name >> 6) & 63, name & 63]
            values = [value.astype(F32) for value in values]
            for place, value in enumerate(values):
                meta = jnp.where((row == token) & (lane == place), value, meta)
        weights = weights_ref[...].astype(F32).reshape(held, 1)
        meta = jnp.where(lane == 6, weights, meta).astype(BF16)
        kinds = [
            jnp.concatenate([
                hidden_ref[:, core * half:(core + 1) * half], meta,
                cotangent_ref[:, core * half + part * quarter:core * half + (part + 1) * quarter]], axis=1)
            for part in range(4) for core in range(2)]
        for device in range(devices):
            core, z, x = device % 2, device // 2 % sizes[2], device // 2 // sizes[2] % sizes[1]
            out_ref[device] = kinds[(x % 2 * 2 + z % 2) * 2 + core]

    return call(
        kernel, "device_blocks", jax.ShapeDtypeStruct((devices, held, kept + quarter), BF16), (),
        [IN_HBM] * 5, WHOLE,
        [
            pltpu.SMEM((held,), I32), pltpu.VMEM((held,), BF16), pltpu.SMEM((held,), I32),
            pltpu.VMEM((held, width), BF16), pltpu.VMEM((held, width), BF16),
            pltpu.SemaphoreType.DMA((5,)),
        ],
        0, 4 * devices * held * half, places, in_hbm(targets), in_hbm(weights), in_hbm(ids), in_hbm(hidden),
        in_hbm(cotangent),
    )


def token_rows(gathered, half):
    chips, held, _ = gathered.shape
    tokens, kept, quarter = chips * held, half + LANES, half // 4

    def kernel(gathered_ref, hidden_ref, quarter_ref, info_ref):
        hidden_ref[...] = gathered_ref[:, :, :half].reshape(tokens, half)
        quarter_ref[...] = gathered_ref[:, :, kept:].reshape(tokens, quarter)
        rows = jnp.transpose(gathered_ref[:, :, half:kept].reshape(tokens, LANES).astype(F32))
        targets = rows[0:1] * 4096.0 + rows[1:2] * 64.0 + rows[2:3]
        ids = rows[3:4] * 4096.0 + rows[4:5] * 64.0 + rows[5:6]
        info_ref[...] = jnp.concatenate([targets, ids, rows[6:7], jnp.zeros((5, tokens), F32)], axis=0)

    return call(
        kernel, "token_rows",
        [jax.ShapeDtypeStruct((tokens, half), BF16), jax.ShapeDtypeStruct((tokens, quarter), BF16),
         jax.ShapeDtypeStruct((8, tokens), F32)],
        (), [WHOLE], [WHOLE] * 3, [], 1 << 33, 4 * tokens * half, [], gathered,
    )


def joined_quarters(own, quarters, after):
    tokens, quarter = quarters[0].shape

    def kernel(own_ref, *refs):
        for place, ref in enumerate(refs[:4]):
            first = pl.multiple_of((own_ref[0] ^ place) * quarter, quarter)
            refs[-1][:, pl.ds(first, quarter)] = ref[...]

    return call(
        kernel, "joined_quarters", jax.ShapeDtypeStruct((tokens, 4 * quarter), BF16),
        (), [WHOLE] * 4 + [IN_HBM], WHOLE, [], 0, 16 * tokens * quarter, [own], *quarters, after,
    )


def feature_products(side, left_ref, head_ref, first, blocks):
    count = left_ref.shape[0]
    for block in range(first, first + blocks, 2):
        columns = jnp.concatenate([
            head_ref[:, pl.ds(pl.multiple_of((2 * place + side) * LANES, LANES), LANES)]
            for place in (block, block + 1)], axis=1)
        for line in range(0, count, count // 2):
            lines = slice(line, line + count // 2)
            total = jnp.dot(left_ref[lines, :], columns, preferred_element_type=F32).astype(BF16)
            yield block, lines, total[:, :LANES], total[:, LANES:]


def local_logits(core, start, devices, info, near, far, head_weight):
    tokens = near.shape[0]
    rows, width = head_weight.shape
    half, step = width // 2, 256
    blocks = half // LANES

    def kernel(core_ref, start_ref, info_ref, near_ref, far_ref, head_ref,
               logits_hbm, stats_hbm, left_hbm, away_hbm, last_ref,
               logits_ref, stats_ref, left_ref, away_ref, sems, away_sems):
        other = 1 - core_ref[0]
        near_columns = pl.ds(pl.multiple_of(core_ref[0] * half, half), half)
        far_columns = pl.ds(pl.multiple_of(other * half, half), half)
        left_ref[tokens:, :] = (
            lax.broadcasted_iota(I32, (tokens, rows), 1) + start_ref[0]
            == jnp.transpose(info_ref[...])[:, 0:1].astype(I32)).astype(F32).astype(BF16)
        for place in range(0, rows, step):
            logits_ref[place:place + step, :] = lax.dot_general(
                head_ref[place:place + step, near_columns], near_ref[...], NT, preferred_element_type=F32)
        for place in range(0, rows, step):
            logits_ref[place:place + step, :] += lax.dot_general(
                head_ref[place:place + step, far_columns], far_ref[...], NT, preferred_element_type=F32)
        copies = [pltpu.make_async_copy(logits_ref, logits_hbm, sems.at[0])]
        copies[-1].start()
        logits = logits_ref[...]
        peak = jnp.max(logits, axis=0, keepdims=True)
        powers = jnp.exp(logits - peak)
        total = jnp.sum(powers, axis=0, keepdims=True)
        row = lax.broadcasted_iota(I32, (rows, tokens), 0) + start_ref[0]
        hits = row == info_ref[0:1, :].astype(I32)
        picked = jnp.sum(jnp.where(hits, logits, 0.0), axis=0, keepdims=True)
        last_ref[...] = jnp.concatenate([peak, picked, jnp.zeros((6, tokens), F32)], axis=0)
        local_norm = peak + jnp.log(total)
        loss = jnp.sum(info_ref[2:3, :] * picked, axis=1, keepdims=True)
        block = jnp.concatenate([local_norm, jnp.broadcast_to(loss, (1, LANES))], axis=1)
        stats_ref[...] = jnp.broadcast_to(block[None], stats_ref.shape)
        copies.append(pltpu.make_async_copy(stats_ref, stats_hbm, sems.at[1]))
        copies[-1].start()
        left_ref[:tokens, :] = jnp.transpose(jnp.where(hits, 0.0, powers)).astype(BF16)
        copies.append(pltpu.make_async_copy(left_ref, left_hbm, sems.at[2]))
        copies[-1].start()
        for first in range(0, blocks, 4):
            for block, lines, even, odd in feature_products(other, left_ref, head_ref, first, 4):
                away_ref[block, lines, :] = even
                away_ref[block + 1, lines, :] = odd
            part = pl.ds(first, 4)
            copies.append(pltpu.make_async_copy(away_ref.at[part], away_hbm.at[part], away_sems.at[first // 4]))
            copies[-1].start()
        for copy in copies:
            copy.wait()

    shapes = [
        ((rows, tokens), F32), ((devices, 1, tokens + LANES), F32),
        ((2 * tokens, rows), BF16), ((blocks, 2 * tokens, LANES), BF16),
    ]
    return call(
        kernel, "local_logits",
        [pltpu.HBM(*shape) for shape in shapes] + [jax.ShapeDtypeStruct((8, tokens), F32)],
        (), [WHOLE] * 4, [IN_HBM] * 4 + [WHOLE],
        [pltpu.VMEM(*shape) for shape in shapes]
        + [pltpu.SemaphoreType.DMA((3,)), pltpu.SemaphoreType.DMA((blocks // 4,))],
        8 * tokens * rows * half, 4 * rows * half, [core, start], info, near, far, head_weight,
    )


def feature_partials(core, left, head_weight):
    count, rows = left.shape
    width = head_weight.shape[1]
    blocks = width // (2 * LANES)

    def kernel(core_ref, left_ref, head_hbm, out_hbm, head_ref, out_ref, head_sems, out_sems):
        loads = []
        for block in range(blocks):
            columns = pl.ds(pl.multiple_of((2 * block + core_ref[0]) * LANES, LANES), LANES)
            loads.append(pltpu.make_async_copy(head_hbm.at[:, columns], head_ref.at[block], head_sems.at[block]))
            loads[-1].start()
        stores = []
        for block in range(0, blocks, 2):
            loads[block].wait()
            loads[block + 1].wait()
            columns = jnp.concatenate([head_ref[block], head_ref[block + 1]], axis=1)
            for line in range(0, count, count // 2):
                lines = slice(line, line + count // 2)
                total = jnp.dot(left_ref[lines, :], columns, preferred_element_type=F32).astype(BF16)
                out_ref[block, lines, :] = total[:, :LANES]
                out_ref[block + 1, lines, :] = total[:, LANES:]
            done = pl.ds(block, 2)
            stores.append(pltpu.make_async_copy(out_ref.at[done], out_hbm.at[done], out_sems.at[block // 2]))
            stores[-1].start()
        for store in stores:
            store.wait()

    shape = ((blocks, count, LANES), BF16)
    return call(
        kernel, "feature_partials", pltpu.HBM(*shape), (), [WHOLE, IN_HBM], IN_HBM,
        [
            pltpu.VMEM((blocks, rows, LANES), BF16), pltpu.VMEM(*shape),
            pltpu.SemaphoreType.DMA((blocks,)), pltpu.SemaphoreType.DMA((blocks // 2,)),
        ],
        1 << 35, 2 * rows * width, [core], left, in_hbm(head_weight),
    )


def scaled_pair(stats, info, last, other_last, home, away):
    tokens = info.shape[1]
    blocks = home.shape[0]
    sections = lax.axis_size("y")
    owned = tokens // sections

    def kernel(stats_ref, info_ref, last_ref, other_last_ref, home_hbm, away_hbm, out_hbm, norm_ref, loss_ref,
               home_ref, away_ref, out_ref, in_sems, out_sems):
        loads = []
        for section in range(sections):
            power = pl.ds(section * owned, owned)
            hit = pl.ds(tokens + section * owned, owned)
            loads.append([
                pltpu.make_async_copy(source.at[:, part, :], target.at[:, part, :], in_sems.at[section, place])
                for place, (source, target, part) in enumerate([
                    (home_hbm, home_ref, power), (away_hbm, away_ref, power),
                    (home_hbm, home_ref, hit), (away_hbm, away_ref, hit)])])
            for load in loads[-1]:
                load.start()

        everyone = stats_ref[:, 0, :]
        norms = everyone[:, :tokens]
        peak = jnp.max(norms, axis=0, keepdims=True)
        norm = peak + jnp.log(jnp.sum(jnp.exp(norms - peak), axis=0, keepdims=True))
        weights = info_ref[2:3, :]
        norm_ref[...] = norm
        picked = jnp.sum(everyone[:, tokens:tokens + 1], axis=0, keepdims=True)
        loss_ref[...] = ((jnp.sum(weights * norm, axis=1, keepdims=True) - picked)
                         / jnp.sum(weights, axis=1, keepdims=True))
        target = jnp.minimum(last_ref[1:2, :] + other_last_ref[1:2, :], norm)
        scale = jnp.transpose(jnp.concatenate([
            weights * jnp.exp(last_ref[0:1, :] - norm),
            weights * jnp.exp(other_last_ref[0:1, :] - norm),
            weights * (jnp.exp(target - norm) - 1.0),
            jnp.zeros((5, tokens), F32),
        ], axis=0))
        stores = []
        for section in range(sections):
            for load in loads[section]:
                load.wait()
            power = slice(section * owned, (section + 1) * owned)
            hit = slice(tokens + section * owned, tokens + (section + 1) * owned)
            one, two, three = (
                jnp.broadcast_to(scale[power, place:place + 1], (owned, LANES)) for place in range(3))
            for block in range(blocks):
                value = home_ref[block, power, :].astype(F32) * one + away_ref[block, power, :].astype(F32) * two
                hits = (home_ref[block, hit, :] + away_ref[block, hit, :]).astype(F32)
                out_ref[section * blocks + block] = (value + hits * three).astype(BF16)
            part = pl.ds(section * blocks, blocks)
            stores.append(pltpu.make_async_copy(out_ref.at[part], out_hbm.at[part], out_sems.at[section]))
            stores[-1].start()
        for store in stores:
            store.wait()

    return call(
        kernel, "scaled_pair",
        [
            pltpu.HBM((sections * blocks, owned, LANES), BF16),
            jax.ShapeDtypeStruct((1, tokens), F32),
            jax.ShapeDtypeStruct((1, 1), F32),
        ],
        (), [WHOLE] * 4 + [IN_HBM] * 2, [IN_HBM, WHOLE, WHOLE],
        [
            pltpu.VMEM(home.shape, BF16), pltpu.VMEM(away.shape, BF16),
            pltpu.VMEM((sections * blocks, owned, LANES), BF16),
            pltpu.SemaphoreType.DMA((sections, 4)), pltpu.SemaphoreType.DMA((sections,)),
        ],
        10 * tokens * blocks * LANES, 10 * tokens * blocks * LANES, [],
        stats, info, last, other_last, in_hbm(home), in_hbm(away),
    )


def summed_parts(parts):
    count, rows, width = parts.shape

    def kernel(parts_ref, out_ref):
        out_ref[...] = jnp.sum(parts_ref[...].astype(F32), axis=0).astype(BF16)

    return call(
        kernel, "summed_parts", jax.ShapeDtypeStruct((rows, width), BF16), (), [WHOLE], WHOLE,
        [], count * rows * width, 2 * count * rows * width, [], parts,
    )


def row_gradient(name, make_left, core, start, new_rows, rows, small, near, far, step=1024):
    tokens = near.shape[0]
    half = near.shape[1]
    steps = half // step

    def kernel(core_ref, start_ref, ranges_ref, *refs):
        small_refs, (near_ref, far_ref, out_ref, left_ref) = refs[:len(small)], refs[len(small):]
        index = pl.program_id(0)

        @pl.when(index == 0)
        def _():
            lane_row = lax.broadcasted_iota(I32, (8, rows), 1) + start_ref[0]
            inside = jnp.zeros((8, rows), F32)
            for place in range(new_rows.shape[0]):
                within = (lane_row >= ranges_ref[place, 0]) & (lane_row < ranges_ref[place, 1])
                inside = jnp.where(within, 1.0, inside)
            gate = jnp.transpose(inside)[:, 0:1]
            row = lax.broadcasted_iota(I32, (rows, tokens), 0) + start_ref[0]
            left_ref[...] = jnp.where(gate > 0.0, make_left(row, *small_refs), 0.0).astype(BF16)

        @pl.when(index < steps)
        def _():
            out_ref[...] = jnp.dot(left_ref[...], near_ref[...], preferred_element_type=F32).astype(BF16)

        @pl.when(index >= steps)
        def _():
            out_ref[...] = jnp.dot(left_ref[...], far_ref[...], preferred_element_type=F32).astype(BF16)

    def out_index(i, core, start, ranges):
        is_far = (i >= steps).astype(I32)
        side = core[0] + is_far - 2 * core[0] * is_far
        return (0, side * steps + i - is_far * steps)

    return call(
        kernel, name,
        jax.ShapeDtypeStruct((rows, 2 * half), BF16),
        (2 * steps,),
        [pl.BlockSpec(array.shape, lambda i, core, start, ranges: (0, 0)) for array in small] + [
            pl.BlockSpec((tokens, step), lambda i, core, start, ranges: (0, jnp.minimum(i, steps - 1))),
            pl.BlockSpec((tokens, step), lambda i, core, start, ranges: (0, jnp.maximum(i - steps, 0))),
        ],
        pl.BlockSpec((rows, step), out_index),
        [pltpu.VMEM((rows, tokens), BF16)],
        4 * rows * tokens * half, 4 * rows * half, [core, start, new_rows], *small, near, far,
    )


def slope_left(row, logits_ref, info_ref, norm_ref):
    hits = (row == info_ref[0:1, :].astype(I32)).astype(F32)
    return info_ref[2:3, :] * (jnp.exp(logits_ref[...] - norm_ref[...]) - hits)


def onehot_left(row, info_ref):
    return (row == info_ref[1:2, :].astype(I32)).astype(F32)


def local(hidden, targets, token_weight, head_weight, token_ids, embed_cotangent, new_rows):
    core = lax.axis_index("c")
    chips = lax.axis_size("y") * lax.axis_size("x") * lax.axis_size("z")
    devices = 2 * chips
    voc_rows = head_weight.shape[0]
    device = ((lax.axis_index("y") * lax.axis_size("x") + lax.axis_index("x"))
              * lax.axis_size("z") + lax.axis_index("z")) * 2 + core
    at_core = core[None].astype(I32)
    start = device[None].astype(I32) * voc_rows
    own_quarter = ((lax.axis_index("x") & 1) * 2 + (lax.axis_index("z") & 1))[None].astype(I32)

    sizes = tuple(lax.axis_size(name) for name in CHIPS)
    blocks = device_blocks([at_core, start, own_quarter], targets, token_weight, token_ids, hidden, embed_cotangent, sizes)
    gathered = lax.all_to_all(blocks, ALL, 0, 0, tiled=True)
    near, quarter, info = token_rows(gathered, hidden.shape[1] // 2)
    far = swap_cores(near)
    logits, stats, left, away, last = local_logits(at_core, start, devices, info, near, far, head_weight)

    stats = lax.all_to_all(stats, ALL, 0, 0, tiled=True)
    away = swap_cores(away)
    home = feature_partials(at_core, left, head_weight)
    near_cotangent = joined_quarters(own_quarter, quarters_around(quarter), last)
    far_cotangent = swap_cores(near_cotangent)

    pair, norm, loss = scaled_pair(stats, info, last, swap_cores(last), home, away)
    grad_hidden = summed_parts(lax.all_to_all(pair, CHIPS, 0, 0, tiled=True))

    grad_head = row_gradient(
        "grad_head", slope_left, at_core, start, new_rows, voc_rows, [logits, info, norm], near, far)
    grad_embed = row_gradient(
        "grad_embed", onehot_left, at_core, start, new_rows, voc_rows, [info], near_cotangent, far_cotangent)
    return (loss[0, 0], grad_hidden, grad_head, grad_embed)


def solution(mesh):
    grid = Mesh(mesh.devices.reshape(4, 4, 4, 2), ALL)
    rows = P(ALL)
    in_specs = (P(ALL, None), rows, rows, P(ALL, None), rows, P(ALL, None), P())
    out_specs = (P(), P("y", ("x", "z", "c")), P(ALL, None), P(ALL, None))
    return jax.shard_map(local, mesh=grid, in_specs=in_specs, out_specs=out_specs, check_vma=False)
```

```python
import jax
import jax.numpy as jnp
from jax import lax
from jax.experimental import pallas as pl
from jax.experimental.pallas import tpu as pltpu
from jax.sharding import Mesh, PartitionSpec as P

CHIPS = ("y", "x", "z")
ALL = ("y", "x", "z", "c")
LANES = 128
VMEM_LIMIT = 24 * 1024 * 1024
F32, BF16, I32 = jnp.float32, jnp.bfloat16, jnp.int32
NT = (((1,), (1,)), ((), ()))
WHOLE = pl.BlockSpec(memory_space=pltpu.VMEM)
IN_HBM = pl.BlockSpec(memory_space=pltpu.HBM)


def call(kernel, name, out_shape, grid, in_specs, out_specs, scratch, flops, moved, scalars, *arrays):
    return pl.pallas_call(
        kernel,
        name=name,
        out_shape=out_shape,
        grid_spec=pltpu.PrefetchScalarGridSpec(
            num_scalar_prefetch=len(scalars),
            grid=grid,
            in_specs=in_specs,
            out_specs=out_specs,
            scratch_shapes=scratch,
        ),
        compiler_params=pltpu.CompilerParams(vmem_limit_bytes=VMEM_LIMIT),
        cost_estimate=pl.CostEstimate(flops=flops, bytes_accessed=moved, transcendentals=0),
    )(*scalars, *arrays)


def in_hbm(value):
    return pltpu.with_memory_space_constraint(value, pltpu.HBM)


def swap_cores(value):
    return lax.ppermute(value, "c", [(0, 1), (1, 0)])


def quarters_around(value):
    count = lax.axis_size("x") * lax.axis_size("z")
    bits = [0, 1, lax.axis_size("z"), lax.axis_size("z") + 1]
    return [value] + [
        lax.ppermute(value, ("x", "z"), [(i, i ^ bit) for i in range(count)]) for bit in bits[1:]]


def device_blocks(places, targets, weights, ids, hidden, cotangent, sizes):
    held, width = hidden.shape
    half, quarter = width // 2, width // 8
    kept = half + LANES
    devices = 2 * sizes[0] * sizes[1] * sizes[2]

    def kernel(core_ref, start_ref, quarter_ref, targets_hbm, weights_hbm, ids_hbm, hidden_hbm, cotangent_hbm, out_ref,
               targets_ref, weights_ref, ids_ref, hidden_ref, cotangent_ref, sems):
        pairs = [(targets_hbm, targets_ref), (ids_hbm, ids_ref), (weights_hbm, weights_ref),
                 (hidden_hbm, hidden_ref), (cotangent_hbm, cotangent_ref)]
        copies = [pltpu.make_async_copy(source, target, sems.at[place])
                  for place, (source, target) in enumerate(pairs)]
        for copy in copies:
            copy.start()
        for copy in copies:
            copy.wait()
        row = lax.broadcasted_iota(I32, (held, LANES), 0)
        lane = lax.broadcasted_iota(I32, (held, LANES), 1)
        meta = jnp.zeros((held, LANES), F32)
        for token in range(held):
            target, name = targets_ref[token], ids_ref[token]
            values = [(target >> 12) & 63, (target >> 6) & 63, target & 63,
                      (name >> 12) & 63, (name >> 6) & 63, name & 63]
            values = [value.astype(F32) for value in values]
            for place, value in enumerate(values):
                meta = jnp.where((row == token) & (lane == place), value, meta)
        weights = weights_ref[...].astype(F32).reshape(held, 1)
        meta = jnp.where(lane == 6, weights, meta).astype(BF16)
        kinds = [
            jnp.concatenate([
                hidden_ref[:, core * half:(core + 1) * half], meta,
                cotangent_ref[:, core * half + part * quarter:core * half + (part + 1) * quarter]], axis=1)
            for part in range(4) for core in range(2)]
        for device in range(devices):
            core, z, x = device % 2, device // 2 % sizes[2], device // 2 // sizes[2] % sizes[1]
            out_ref[device] = kinds[(x % 2 * 2 + z % 2) * 2 + core]

    return call(
        kernel, "device_blocks", jax.ShapeDtypeStruct((devices, held, kept + quarter), BF16), (),
        [IN_HBM] * 5, WHOLE,
        [
            pltpu.SMEM((held,), I32), pltpu.VMEM((held,), BF16), pltpu.SMEM((held,), I32),
            pltpu.VMEM((held, width), BF16), pltpu.VMEM((held, width), BF16),
            pltpu.SemaphoreType.DMA((5,)),
        ],
        0, 4 * devices * held * half, places, in_hbm(targets), in_hbm(weights), in_hbm(ids), in_hbm(hidden),
        in_hbm(cotangent),
    )


def token_rows(gathered, half):
    chips, held, _ = gathered.shape
    tokens, kept, quarter = chips * held, half + LANES, half // 4

    def kernel(gathered_ref, hidden_ref, quarter_ref, info_ref):
        hidden_ref[...] = gathered_ref[:, :, :half].reshape(tokens, half)
        quarter_ref[...] = gathered_ref[:, :, kept:].reshape(tokens, quarter)
        rows = jnp.transpose(gathered_ref[:, :, half:kept].reshape(tokens, LANES).astype(F32))
        targets = rows[0:1] * 4096.0 + rows[1:2] * 64.0 + rows[2:3]
        ids = rows[3:4] * 4096.0 + rows[4:5] * 64.0 + rows[5:6]
        info_ref[...] = jnp.concatenate([targets, ids, rows[6:7], jnp.zeros((5, tokens), F32)], axis=0)

    return call(
        kernel, "token_rows",
        [jax.ShapeDtypeStruct((tokens, half), BF16), jax.ShapeDtypeStruct((tokens, quarter), BF16),
         jax.ShapeDtypeStruct((8, tokens), F32)],
        (), [WHOLE], [WHOLE] * 3, [], 1 << 33, 4 * tokens * half, [], gathered,
    )


def joined_quarters(own, quarters, after):
    tokens, quarter = quarters[0].shape

    def kernel(own_ref, *refs):
        for place, ref in enumerate(refs[:4]):
            first = pl.multiple_of((own_ref[0] ^ place) * quarter, quarter)
            refs[-1][:, pl.ds(first, quarter)] = ref[...]

    return call(
        kernel, "joined_quarters", jax.ShapeDtypeStruct((tokens, 4 * quarter), BF16),
        (), [WHOLE] * 4 + [IN_HBM], WHOLE, [], 0, 16 * tokens * quarter, [own], *quarters, after,
    )


def feature_products(side, left_ref, head_ref, first, blocks):
    count = left_ref.shape[0]
    for block in range(first, first + blocks, 2):
        columns = jnp.concatenate([
            head_ref[:, pl.ds(pl.multiple_of((2 * place + side) * LANES, LANES), LANES)]
            for place in (block, block + 1)], axis=1)
        for line in range(0, count, count // 2):
            lines = slice(line, line + count // 2)
            total = jnp.dot(left_ref[lines, :], columns, preferred_element_type=F32).astype(BF16)
            yield block, lines, total[:, :LANES], total[:, LANES:]


def local_logits(core, start, devices, info, near, far, head_weight):
    tokens = near.shape[0]
    rows, width = head_weight.shape
    half, step = width // 2, 512
    blocks = half // LANES

    def kernel(core_ref, start_ref, info_ref, near_ref, far_ref, head_ref,
               logits_hbm, stats_hbm, left_hbm, away_hbm, last_ref,
               logits_ref, stats_ref, left_ref, away_ref, sems, away_sems):
        other = 1 - core_ref[0]
        near_columns = pl.ds(pl.multiple_of(core_ref[0] * half, half), half)
        far_columns = pl.ds(pl.multiple_of(other * half, half), half)
        left_ref[tokens:, :] = (
            lax.broadcasted_iota(I32, (tokens, rows), 1) + start_ref[0]
            == jnp.transpose(info_ref[...])[:, 0:1].astype(I32)).astype(F32).astype(BF16)
        for place in range(0, rows, step):
            logits_ref[place:place + step, :] = lax.dot_general(
                head_ref[place:place + step, near_columns], near_ref[...], NT, preferred_element_type=F32)
        for place in range(0, rows, step):
            logits_ref[place:place + step, :] += lax.dot_general(
                head_ref[place:place + step, far_columns], far_ref[...], NT, preferred_element_type=F32)
        copies = [pltpu.make_async_copy(logits_ref, logits_hbm, sems.at[0])]
        copies[-1].start()
        logits = logits_ref[...]
        peak = jnp.max(logits, axis=0, keepdims=True)
        powers = jnp.exp(logits - peak)
        total = jnp.sum(powers, axis=0, keepdims=True)
        row = lax.broadcasted_iota(I32, (rows, tokens), 0) + start_ref[0]
        hits = row == info_ref[0:1, :].astype(I32)
        picked = jnp.sum(jnp.where(hits, logits, 0.0), axis=0, keepdims=True)
        last_ref[...] = jnp.concatenate([peak, picked, jnp.zeros((6, tokens), F32)], axis=0)
        local_norm = peak + jnp.log(total)
        loss = jnp.sum(info_ref[2:3, :] * picked, axis=1, keepdims=True)
        block = jnp.concatenate([local_norm, jnp.broadcast_to(loss, (1, LANES))], axis=1)
        stats_ref[...] = jnp.broadcast_to(block[None], stats_ref.shape)
        copies.append(pltpu.make_async_copy(stats_ref, stats_hbm, sems.at[1]))
        copies[-1].start()
        left_ref[:tokens, :] = jnp.transpose(jnp.where(hits, 0.0, powers)).astype(BF16)
        copies.append(pltpu.make_async_copy(left_ref, left_hbm, sems.at[2]))
        copies[-1].start()
        for first in range(0, blocks, 4):
            for block, lines, even, odd in feature_products(other, left_ref, head_ref, first, 4):
                away_ref[block, lines, :] = even
                away_ref[block + 1, lines, :] = odd
            part = pl.ds(first, 4)
            copies.append(pltpu.make_async_copy(away_ref.at[part], away_hbm.at[part], away_sems.at[first // 4]))
            copies[-1].start()
        for copy in copies:
            copy.wait()

    shapes = [
        ((rows, tokens), F32), ((devices, 1, tokens + LANES), F32),
        ((2 * tokens, rows), BF16), ((blocks, 2 * tokens, LANES), BF16),
    ]
    return call(
        kernel, "local_logits",
        [pltpu.HBM(*shape) for shape in shapes] + [jax.ShapeDtypeStruct((8, tokens), F32)],
        (), [WHOLE] * 4, [IN_HBM] * 4 + [WHOLE],
        [pltpu.VMEM(*shape) for shape in shapes]
        + [pltpu.SemaphoreType.DMA((3,)), pltpu.SemaphoreType.DMA((blocks // 4,))],
        8 * tokens * rows * half, 4 * rows * half, [core, start], info, near, far, head_weight,
    )


def feature_partials(core, left, head_weight):
    count, rows = left.shape
    width = head_weight.shape[1]
    blocks = width // (2 * LANES)
    step = 1024
    held = step // (2 * LANES)

    def kernel(core_ref, left_ref, head_hbm, out_hbm, head_ref, out_ref, head_sems, out_sems):
        loads = [
            pltpu.make_async_copy(head_hbm.at[:, pl.ds(place * step, step)], head_ref.at[place], head_sems.at[place])
            for place in range(width // step)]
        for load in loads:
            load.start()
        stores = []
        for place, load in enumerate(loads):
            load.wait()
            for block, lines, even, odd in feature_products(core_ref[0], left_ref, head_ref.at[place], 0, held):
                out_ref[place * held + block, lines, :] = even
                out_ref[place * held + block + 1, lines, :] = odd
            part = pl.ds(place * held, held)
            stores.append(pltpu.make_async_copy(out_ref.at[part], out_hbm.at[part], out_sems.at[place]))
            stores[-1].start()
        for store in stores:
            store.wait()

    shape = ((blocks, count, LANES), BF16)
    return call(
        kernel, "feature_partials", pltpu.HBM(*shape), (), [WHOLE, IN_HBM], IN_HBM,
        [
            pltpu.VMEM((width // step, rows, step), BF16), pltpu.VMEM(*shape),
            pltpu.SemaphoreType.DMA((width // step,)), pltpu.SemaphoreType.DMA((width // step,)),
        ],
        1 << 35, 2 * rows * width, [core], left, in_hbm(head_weight),
    )


def scaled_pair(stats, info, last, other_last, home, away):
    tokens = info.shape[1]
    blocks = home.shape[0]
    sections = lax.axis_size("y")
    owned = tokens // sections

    def kernel(stats_ref, info_ref, last_ref, other_last_ref, home_hbm, away_hbm, out_hbm, norm_ref, loss_ref,
               home_ref, away_ref, out_ref, in_sems, out_sems):
        loads = []
        for section in range(sections):
            power = pl.ds(section * owned, owned)
            hit = pl.ds(tokens + section * owned, owned)
            loads.append([
                pltpu.make_async_copy(source.at[:, part, :], target.at[:, part, :], in_sems.at[section, place])
                for place, (source, target, part) in enumerate([
                    (home_hbm, home_ref, power), (away_hbm, away_ref, power),
                    (home_hbm, home_ref, hit), (away_hbm, away_ref, hit)])])
            for load in loads[-1]:
                load.start()

        everyone = stats_ref[:, 0, :]
        norms = everyone[:, :tokens]
        peak = jnp.max(norms, axis=0, keepdims=True)
        norm = peak + jnp.log(jnp.sum(jnp.exp(norms - peak), axis=0, keepdims=True))
        weights = info_ref[2:3, :]
        norm_ref[...] = norm
        picked = jnp.sum(everyone[:, tokens:tokens + 1], axis=0, keepdims=True)
        loss_ref[...] = ((jnp.sum(weights * norm, axis=1, keepdims=True) - picked)
                         / jnp.sum(weights, axis=1, keepdims=True))
        target = jnp.minimum(last_ref[1:2, :] + other_last_ref[1:2, :], norm)
        scale = jnp.transpose(jnp.concatenate([
            weights * jnp.exp(last_ref[0:1, :] - norm),
            weights * jnp.exp(other_last_ref[0:1, :] - norm),
            weights * (jnp.exp(target - norm) - 1.0),
            jnp.zeros((5, tokens), F32),
        ], axis=0))
        stores = []
        for section in range(sections):
            for load in loads[section]:
                load.wait()
            power = slice(section * owned, (section + 1) * owned)
            hit = slice(tokens + section * owned, tokens + (section + 1) * owned)
            one, two, three = (
                jnp.broadcast_to(scale[power, place:place + 1], (owned, LANES)) for place in range(3))
            for block in range(blocks):
                value = home_ref[block, power, :].astype(F32) * one + away_ref[block, power, :].astype(F32) * two
                hits = (home_ref[block, hit, :] + away_ref[block, hit, :]).astype(F32)
                out_ref[section * blocks + block] = (value + hits * three).astype(BF16)
            part = pl.ds(section * blocks, blocks)
            stores.append(pltpu.make_async_copy(out_ref.at[part], out_hbm.at[part], out_sems.at[section]))
            stores[-1].start()
        for store in stores:
            store.wait()

    return call(
        kernel, "scaled_pair",
        [
            pltpu.HBM((sections * blocks, owned, LANES), BF16),
            jax.ShapeDtypeStruct((1, tokens), F32),
            jax.ShapeDtypeStruct((1, 1), F32),
        ],
        (), [WHOLE] * 4 + [IN_HBM] * 2, [IN_HBM, WHOLE, WHOLE],
        [
            pltpu.VMEM(home.shape, BF16), pltpu.VMEM(away.shape, BF16),
            pltpu.VMEM((sections * blocks, owned, LANES), BF16),
            pltpu.SemaphoreType.DMA((sections, 4)), pltpu.SemaphoreType.DMA((sections,)),
        ],
        10 * tokens * blocks * LANES, 10 * tokens * blocks * LANES, [],
        stats, info, last, other_last, in_hbm(home), in_hbm(away),
    )


def summed_parts(parts):
    count, rows, width = parts.shape

    def kernel(parts_ref, out_ref):
        out_ref[...] = jnp.sum(parts_ref[...].astype(F32), axis=0).astype(BF16)

    return call(
        kernel, "summed_parts", jax.ShapeDtypeStruct((rows, width), BF16), (), [WHOLE], WHOLE,
        [], count * rows * width, 2 * count * rows * width, [], parts,
    )


def row_gradient(name, make_left, core, start, new_rows, rows, small, near, far, step=1024):
    tokens = near.shape[0]
    half = near.shape[1]
    steps = half // step

    def kernel(core_ref, start_ref, ranges_ref, *refs):
        small_refs, (near_ref, far_ref, out_ref, left_ref) = refs[:len(small)], refs[len(small):]
        index = pl.program_id(0)

        @pl.when(index == 0)
        def _():
            lane_row = lax.broadcasted_iota(I32, (8, rows), 1) + start_ref[0]
            inside = jnp.zeros((8, rows), F32)
            for place in range(new_rows.shape[0]):
                within = (lane_row >= ranges_ref[place, 0]) & (lane_row < ranges_ref[place, 1])
                inside = jnp.where(within, 1.0, inside)
            gate = jnp.transpose(inside)[:, 0:1]
            row = lax.broadcasted_iota(I32, (rows, tokens), 0) + start_ref[0]
            left_ref[...] = jnp.where(gate > 0.0, make_left(row, *small_refs), 0.0).astype(BF16)

        @pl.when(index < steps)
        def _():
            out_ref[...] = jnp.dot(left_ref[...], near_ref[...], preferred_element_type=F32).astype(BF16)

        @pl.when(index >= steps)
        def _():
            out_ref[...] = jnp.dot(left_ref[...], far_ref[...], preferred_element_type=F32).astype(BF16)

    def out_index(i, core, start, ranges):
        is_far = (i >= steps).astype(I32)
        side = core[0] + is_far - 2 * core[0] * is_far
        return (0, side * steps + i - is_far * steps)

    return call(
        kernel, name,
        jax.ShapeDtypeStruct((rows, 2 * half), BF16),
        (2 * steps,),
        [pl.BlockSpec(array.shape, lambda i, core, start, ranges: (0, 0)) for array in small] + [
            pl.BlockSpec((tokens, step), lambda i, core, start, ranges: (0, jnp.minimum(i, steps - 1))),
            pl.BlockSpec((tokens, step), lambda i, core, start, ranges: (0, jnp.maximum(i - steps, 0))),
        ],
        pl.BlockSpec((rows, step), out_index),
        [pltpu.VMEM((rows, tokens), BF16)],
        4 * rows * tokens * half, 4 * rows * half, [core, start, new_rows], *small, near, far,
    )


def slope_left(row, logits_ref, info_ref, norm_ref):
    hits = (row == info_ref[0:1, :].astype(I32)).astype(F32)
    return info_ref[2:3, :] * (jnp.exp(logits_ref[...] - norm_ref[...]) - hits)


def onehot_left(row, info_ref):
    return (row == info_ref[1:2, :].astype(I32)).astype(F32)


def local(hidden, targets, token_weight, head_weight, token_ids, embed_cotangent, new_rows):
    core = lax.axis_index("c")
    chips = lax.axis_size("y") * lax.axis_size("x") * lax.axis_size("z")
    devices = 2 * chips
    voc_rows = head_weight.shape[0]
    device = ((lax.axis_index("y") * lax.axis_size("x") + lax.axis_index("x"))
              * lax.axis_size("z") + lax.axis_index("z")) * 2 + core
    at_core = core[None].astype(I32)
    start = device[None].astype(I32) * voc_rows
    own_quarter = ((lax.axis_index("x") & 1) * 2 + (lax.axis_index("z") & 1))[None].astype(I32)

    sizes = tuple(lax.axis_size(name) for name in CHIPS)
    blocks = device_blocks([at_core, start, own_quarter], targets, token_weight, token_ids, hidden, embed_cotangent, sizes)
    gathered = lax.all_to_all(blocks, ALL, 0, 0, tiled=True)
    near, quarter, info = token_rows(gathered, hidden.shape[1] // 2)
    far = swap_cores(near)
    logits, stats, left, away, last = local_logits(at_core, start, devices, info, near, far, head_weight)

    stats = lax.all_to_all(stats, ALL, 0, 0, tiled=True)
    away = swap_cores(away)
    home = feature_partials(at_core, left, head_weight)
    near_cotangent = joined_quarters(own_quarter, quarters_around(quarter), last)
    far_cotangent = swap_cores(near_cotangent)

    pair, norm, loss = scaled_pair(stats, info, last, swap_cores(last), home, away)
    grad_hidden = summed_parts(lax.all_to_all(pair, CHIPS, 0, 0, tiled=True))

    grad_head = row_gradient(
        "grad_head", slope_left, at_core, start, new_rows, voc_rows, [logits, info, norm], near, far)
    grad_embed = row_gradient(
        "grad_embed", onehot_left, at_core, start, new_rows, voc_rows, [info], near_cotangent, far_cotangent)
    return (loss[0, 0], grad_hidden, grad_head, grad_embed)


def solution(mesh):
    grid = Mesh(mesh.devices.reshape(4, 4, 4, 2), ALL)
    rows = P(ALL)
    in_specs = (P(ALL, None), rows, rows, P(ALL, None), rows, P(ALL, None), P())
    out_specs = (P(), P("y", ("x", "z", "c")), P(ALL, None), P(ALL, None))
    return jax.shard_map(local, mesh=grid, in_specs=in_specs, out_specs=out_specs, check_vma=False)
```
